512 devices in a mesh: blk: 64 (over x_lo, z, core), tensor: 8 (over y, x_hi).
Axes of the slice: x: 4 (x_hi: 2, x_lo: 2; x = x_hi * 2 + x_lo), y: 4, z: 16, core: 2. Of those that a mesh axis runs over, the one named last changes fastest.
Arguments:
- weights: float32 [16384, 18944], P('blk', 'tensor'), may hold values from -6 to 6
- warm_q: float32 [64, 18944, 16], P('blk', 'tensor'), may hold values from -6 to 6
Outputs:
- new_weights: float32 [16384, 18944], P('blk', 'tensor')
- next_q: float32 [64, 18944, 16], P('blk', 'tensor')
The draws below stay inside these ranges and needn't reach their ends.
All inputs are finite; a program needn't handle non-finite values.
Results may differ from the reference program's by a relative error of at most 0.0003.
Values sent between devices are 32-bit elements; how exact they have to be, the bound alone decides.
No kernel may reach another device: no remote copies, remote signals or barrier semaphores. Data moves between devices by JAX's collectives and lax.ppermute only.
A program may use at most 64 MiB of HBM per device.

```python
import jax
import jax.numpy as jnp
from jax import lax

FF = 18944
ROWS = 256
RANK = 16
REPLICAS = 64


def block_levels(key, extent, split, smallest, top_value):
    loudness, own = 1.0, jax.random.fold_in(key, 6)
    for position, shards_of in split:
        heights = jnp.exp(jax.random.uniform(jax.random.fold_in(own, position), (shards_of,), jnp.float32, smallest / len(split), top_value / len(split)))
        loudness = loudness * jnp.repeat(heights, extent[position] // shards_of).reshape([-1 if axis == position else 1 for axis in range(len(extent))])
    return loudness


def bell_draw(own_key, shape, deviation, bound, pieces=(), kind=jnp.bfloat16):
    drawn = deviation * jax.random.normal(own_key, shape, jnp.float32)
    if pieces:
        drawn = drawn * block_levels(own_key, shape, pieces, -0.22, 0.18)
    return jnp.clip(drawn, -bound, bound).astype(kind)


def setup_inputs(seed: int = 0) -> dict:
    key_list = jax.random.split(jax.random.key(seed), 3)
    return {
        "weights": bell_draw(key_list[0], (REPLICAS * ROWS, FF), 1.0, 6.0, ((0, 64), (1, 8)), jnp.float32),
        "warm_q": bell_draw(key_list[1], (REPLICAS, FF, RANK), 1.0, 6.0, ((0, 64), (1, 8)), jnp.float32),
    }


HIGH = lax.Precision.HIGHEST

def orthonormal(matrix):
    gram = jnp.dot(matrix.T, matrix, precision=HIGH)
    lower = jnp.linalg.cholesky(gram)
    return lax.linalg.triangular_solve(lower, matrix, left_side=False, lower=True, transpose_a=True)

def reference(weights, warm_q):
    stacked = weights.reshape(REPLICAS, ROWS, FF)

    def edge(index):
        after = (index + 1) % REPLICAS
        mine = stacked[index]
        other = stacked[after]
        start = warm_q[index]
        rows = orthonormal(jnp.dot(mine, start, precision=HIGH) - jnp.dot(other, start, precision=HIGH))
        cols = jnp.dot(mine.T, rows, precision=HIGH) - jnp.dot(other.T, rows, precision=HIGH)
        rows = orthonormal(jnp.dot(mine, cols, precision=HIGH) - jnp.dot(other, cols, precision=HIGH))
        cols = jnp.dot(mine.T, rows, precision=HIGH) - jnp.dot(other.T, rows, precision=HIGH)
        return (rows, cols)
    indices = jnp.arange(REPLICAS, dtype=jnp.int32)
    rows_all, cols_all = lax.map(edge, indices)

    def update(index):
        before = (index + REPLICAS - 1) % REPLICAS
        change = jnp.dot(rows_all[index], cols_all[index].T, precision=HIGH)
        change = change - jnp.dot(rows_all[before], cols_all[before].T, precision=HIGH)
        return stacked[index] - 0.5 * change
    new_weights = lax.map(update, indices)
    return (new_weights.reshape(REPLICAS * ROWS, FF), cols_all)
```

```python
import jax
import jax.numpy as jnp
from jax import lax
from jax.experimental import pallas as pl
from jax.experimental.pallas import tpu as pltpu
from jax.sharding import PartitionSpec as P

HIGH = lax.Precision.HIGHEST
step_size = 0.5


def swapped(block, partner):
    devices = lax.axis_size("blk")
    return lax.ppermute(block, "blk", [(i, partner(i) % devices) for i in range(devices)])


def take_left(block):
    return swapped(block, lambda i: i + 1)


def take_chip(block):
    return swapped(block, lambda i: i ^ 1)


def take_z(block):
    return swapped(block, lambda i: ((i + 1) ^ 1) - 1)


def orth_kernel(parts_ref, out_ref):
    total = parts_ref[0]
    for k in range(1, parts_ref.shape[0]):
        total = total + parts_ref[k]
    both = total.shape[0]
    rank = both // 2
    gram = lax.dot_general(
        total, total, (((1,), (1,)), ((), ())), precision=HIGH, preferred_element_type=jnp.float32
    )
    row = lax.broadcasted_iota(jnp.int32, (rank, 1), 0)
    for edge in range(2):
        rows = slice(edge * rank, (edge + 1) * rank)
        g = gram[rows, rows]
        m = total[rows]
        for j in range(rank):
            inverse = 1.0 / g[j : j + 1, j : j + 1]
            factor = jnp.where(row > j, g[:, j : j + 1] * inverse, 0.0)
            g_row, m_row = g[j : j + 1], m[j : j + 1]
            scale = jnp.where(row == j, lax.rsqrt(g[j : j + 1, j : j + 1]), 1.0)
            g = g - factor * g_row
            m = (m - factor * m_row) * scale
        out_ref[rows] = m


def orthonormal(parts):
    return pl.pallas_call(
        orth_kernel,
        out_shape=jax.ShapeDtypeStruct(parts.shape[1:], jnp.float32),
        in_specs=[pl.BlockSpec(memory_space=pltpu.VMEM)],
        out_specs=pl.BlockSpec(memory_space=pltpu.VMEM),
    )(parts)


def gathered(block):
    ranks = lax.axis_size("tensor")
    copies = jnp.broadcast_to(block[None], (ranks, *block.shape))
    return lax.all_to_all(copies, "tensor", 0, 0, tiled=True)


def shards(weights, warm_q):
    own = weights.T
    start = warm_q[0].T
    rank = start.shape[0]
    even = lax.axis_index("blk") % 2 == 0
    left = take_left(start)
    first = own.shape[0] // 512 * 128
    near_z = [take_z(own[:first])]
    q_chip = jnp.where(even, start, left)
    q_z = jnp.where(even, left, start)
    mine = jnp.dot(jnp.concatenate([q_chip, q_z], axis=0), own, precision=HIGH)
    theirs_z = take_z(mine[rank:])
    theirs_chip = take_chip(mine[:rank])
    rest, mine = lax.optimization_barrier((own[first:], mine))
    near_z = jnp.concatenate(near_z + [take_z(rest)], axis=0)
    near_chip = take_chip(lax.optimization_barrier((own, mine))[0])
    rows = mine - jnp.concatenate([theirs_chip, theirs_z], axis=0)
    basis = orthonormal(gathered(rows))
    d_chip, d_z = own - near_chip, own - near_z

    def columns(basis):
        c = lax.dot_general(basis[:rank], d_chip, (((1,), (1,)), ((), ())), precision=HIGH)
        z = lax.dot_general(basis[rank:], d_z, (((1,), (1,)), ((), ())), precision=HIGH)
        return c, z

    cols_chip, cols_z = columns(basis)
    rows = jnp.concatenate(
        [jnp.dot(cols_chip, d_chip, precision=HIGH), jnp.dot(cols_z, d_z, precision=HIGH)], axis=0
    )
    basis = orthonormal(gathered(rows))
    cols_chip, cols_z = columns(basis)
    change = lax.dot_general(
        jnp.concatenate([cols_chip, cols_z], axis=0), basis, (((0,), (0,)), ((), ())), precision=HIGH
    )
    new = own - step_size * change
    return new.T, jnp.where(even, cols_chip, cols_z).T[None]


def solution(mesh):
    in_specs = (P("blk", "tensor"), P("blk", "tensor", None))
    out_specs = (P("blk", "tensor"), P("blk", "tensor", None))
    return jax.shard_map(shards, mesh=mesh, in_specs=in_specs, out_specs=out_specs, check_vma=False)
```

```python
import functools

import jax
import jax.numpy as jnp
from jax import lax
from jax.experimental import pallas as pl
from jax.experimental.pallas import tpu as pltpu
from jax.sharding import PartitionSpec as P

HIGH = lax.Precision.HIGHEST
f32 = jnp.float32
bf16 = jnp.bfloat16
step_size = 0.5
VMEM = pl.BlockSpec(memory_space=pltpu.VMEM)
HBM = pl.BlockSpec(memory_space=pl.ANY)
NN = (((1,), (0,)), ((), ()))
NT = (((1,), (1,)), ((), ()))


def swapped(block, partner):
    devices = lax.axis_size("blk")
    return lax.ppermute(block, "blk", [(i, partner(i) % devices) for i in range(devices)])


def take_left(block):
    return swapped(block, lambda i: i + 1)


def take_chip(block):
    return swapped(block, lambda i: i ^ 1)


def take_z(block):
    return swapped(block, lambda i: ((i + 1) ^ 1) - 1)


def is_even():
    return lax.rem(lax.axis_index("blk"), 2) == 0


def planes(x):
    one = x.astype(bf16)
    rest = x - one.astype(f32)
    two = rest.astype(bf16)
    return one, two, (rest - two.astype(f32)).astype(bf16)


def dot(a, b, dims=NN):
    return lax.dot_general(a, b, dims, preferred_element_type=f32)


def product(small, large):
    rows = small[0].shape[0]
    a = dot(jnp.concatenate(small, axis=0), large[0])
    b = dot(jnp.concatenate(small[:2], axis=0), large[1])
    c = dot(small[0], large[2])
    return a[:rows] + ((a[rows : 2 * rows] + b[:rows]) + (a[2 * rows :] + b[rows:] + c))


def tiles(extent, tile):
    return [(at, min(tile, extent - at)) for at in range(0, extent, tile)]


def orthonormal_rows(total):
    both, width = total.shape
    rank = both // 2
    gram = lax.dot_general(total, total, NT, precision=HIGH, preferred_element_type=f32)
    g = jnp.stack([gram[:rank, :rank], gram[rank:, rank:]])
    m = total.reshape(2, rank, width)
    row = lax.broadcasted_iota(jnp.int32, (2, rank, 1), 1)
    scale = jnp.ones((2, rank, 1), f32)
    for j in range(rank):
        pivot = g[:, j : j + 1, j : j + 1]
        factor = jnp.where(row > j, g[:, :, j : j + 1] * (1.0 / pivot), 0.0)
        scale = jnp.where(row == j, lax.rsqrt(pivot), scale)
        m = m - factor * m[:, j : j + 1]
        g = g - factor * g[:, j : j + 1]
    return (m * scale).reshape(both, width)


def summed(parts_ref):
    total = parts_ref[0]
    for k in range(1, parts_ref.shape[0]):
        total = total + parts_ref[k]
    return total


def rows_kernel(start_ref, left_ref, own_ref, near_chip_ref, chip_ref, z_ref):
    even = is_even()
    rank, width = z_ref.shape
    chip = jnp.zeros((rank, width), f32)
    z = jnp.zeros((rank, width), f32)
    for at, size in tiles(own_ref.shape[0], 256):
        part = pl.ds(at, size)
        start, left, own = start_ref[:, part], left_ref[:, part], own_ref[part]
        chip = chip + product(planes(jnp.where(even, start, left)), planes(own - near_chip_ref[part]))
        z = z + product(planes(jnp.where(even, left, start)), planes(own))
    for k in range(chip_ref.shape[0]):
        chip_ref[k] = chip
    z_ref[...] = z


def basis_kernel(parts_ref, out_ref):
    out_ref[...] = orthonormal_rows(summed(parts_ref))


def right_sides(basis):
    rank = basis.shape[0] // 2
    zero = jnp.zeros((rank, basis.shape[1]), f32)
    sides = []
    for edge in range(2):
        p = [x.astype(f32) for x in planes(basis[edge * rank : (edge + 1) * rank])]
        for kept in (3, 2, 1):
            groups = []
            for k in range(4):
                x = p[k] if k < kept else zero
                groups += [x, zero] if edge == 0 else [zero, x]
            sides.append(jnp.transpose(jnp.concatenate(groups, axis=0)).astype(bf16))
    return jnp.concatenate(sides, axis=0)


def columns(differences, right):
    left = jnp.concatenate([p for d in differences for p in d], axis=1)
    groups = dot(left, right)
    groups = groups + pltpu.roll(groups, 64, 1)
    return groups + pltpu.roll(groups, 32, 1)


def power_kernel(basis_ref, own_ref, near_chip_ref, first_ref, rest_ref, out_ref):
    both, width = basis_ref.shape
    rank = both // 2
    right = right_sides(basis_ref[...])
    totals = [jnp.zeros((rank, width), f32)] * 2
    for at, size in tiles(own_ref.shape[0], 640):
        part = pl.ds(at, size)
        first = first_ref.shape[0]
        near_z = first_ref[part] if at < first else rest_ref[pl.ds(at - first, size)]
        own = own_ref[part]
        differences = [planes(own - near_chip_ref[part]), planes(own - near_z)]
        cols = jnp.transpose(columns(differences, right))[:both]
        for edge in range(2):
            c = planes(cols[edge * rank : (edge + 1) * rank])
            totals[edge] = totals[edge] + product(c, differences[edge])
    total = jnp.concatenate(totals, axis=0)
    for k in range(out_ref.shape[0]):
        out_ref[k] = total


def update_kernel(parts_ref, own_ref, near_chip_ref, first_ref, rest_ref, new_ref, cols_ref, held, sems):
    even = is_even()
    basis = orthonormal_rows(summed(parts_ref))
    both, width = basis.shape
    rank = both // 2
    right = right_sides(basis)
    b = planes(-step_size * basis)
    zero = jnp.zeros_like(b[0])
    change_right = jnp.concatenate([b[0], b[1], b[2], b[0], b[1], b[0], zero, zero], axis=0)
    copies = []
    for k, (at, size) in enumerate(tiles(own_ref.shape[0], 640)):
        part = pl.ds(at, size)
        first = first_ref.shape[0]
        near_z = first_ref[part] if at < first else rest_ref[pl.ds(at - first, size)]
        own = own_ref[part]
        cols = columns([planes(own - near_chip_ref[part]), planes(own - near_z)], right)
        turned = jnp.transpose(cols)
        cols_ref[:, part] = jnp.where(even, turned[:rank], turned[rank:both])
        group = lax.broadcasted_iota(jnp.int32, cols.shape, 1) // both
        c = planes(cols)
        low = jnp.where(group < 3, c[0].astype(f32), c[1].astype(f32))
        high = jnp.where(group == 0, c[1].astype(f32), c[2].astype(f32))
        left = jnp.concatenate([low, high], axis=1).astype(bf16)
        held[part] = own + dot(left, change_right)
        copy = pltpu.make_async_copy(held.at[part], new_ref.at[part], sems.at[k])
        copy.start()
        copies.append(copy)
    for copy in copies:
        copy.wait()


def call(kernel, name, out_shape, out_specs, cost_us, scratch=(), mib=16):
    return lambda *args: pl.pallas_call(
        kernel,
        out_shape=out_shape,
        in_specs=[VMEM] * len(args),
        out_specs=out_specs,
        scratch_shapes=scratch,
        compiler_params=pltpu.CompilerParams(vmem_limit_bytes=mib * 2**20),
        cost_estimate=pl.CostEstimate(flops=int(cost_us*1.15e9), bytes_accessed=0, transcendentals=0),
        name=name,
    )(*args)


def gathered(copies):
    return lax.all_to_all(copies, "tensor", 0, 0, tiled=True)


COST = dict(rows=8, basis=14, power=4, update=6)
FIRST = 640


def shards(weights, warm_q):
    own = weights.T
    start = warm_q[0].T
    rank, extent = start.shape
    width = own.shape[1]
    ranks = lax.axis_size("tensor")
    shape = lambda *dims: jax.ShapeDtypeStruct(dims, f32)

    left = take_left(start)
    first_z = take_z(own[:FIRST])
    near_chip = take_chip(own)
    chip, z = call(
        rows_kernel, "rows", (shape(ranks, rank, width), shape(rank, width)), (VMEM, VMEM), COST["rows"]
    )(start, left, own, near_chip)
    theirs = take_z(z)
    rest, chip = lax.optimization_barrier((own[FIRST:], chip))
    rest_z = take_z(rest)
    z, first_z = lax.optimization_barrier((z - theirs, first_z))
    rows = jnp.concatenate([chip, jnp.broadcast_to(z[None], chip.shape)], axis=1)
    parts = gathered(rows)
    basis = call(basis_kernel, "basis", shape(2 * rank, width), VMEM, COST["basis"], mib=4)(parts)
    copies = call(power_kernel, "power", shape(ranks, 2 * rank, width), VMEM, COST["power"])(
        basis, own, near_chip, first_z, rest_z
    )
    parts = gathered(copies)
    new, cols = call(
        update_kernel,
        "update",
        (shape(extent, width), shape(rank, extent)),
        (HBM, VMEM),
        COST["update"],
        scratch=[pltpu.VMEM((extent, width), f32), pltpu.SemaphoreType.DMA((len(tiles(extent, 640)),))],
    )(parts, own, near_chip, first_z, rest_z)
    return new.T, cols.T[None]


def solution(mesh):
    in_specs = (P("blk", "tensor"), P("blk", "tensor", None))
    out_specs = (P("blk", "tensor"), P("blk", "tensor", None))
    return jax.shard_map(shards, mesh=mesh, in_specs=in_specs, out_specs=out_specs, check_vma=False)
```

```python
import functools

import jax
import jax.numpy as jnp
from jax import lax
from jax.experimental import pallas as pl
from jax.experimental.pallas import tpu as pltpu
from jax.sharding import PartitionSpec as P

HIGH = lax.Precision.HIGHEST
f32 = jnp.float32
bf16 = jnp.bfloat16
step_size = 0.5
VMEM = pl.BlockSpec(memory_space=pltpu.VMEM)
HBM = pl.BlockSpec(memory_space=pl.ANY)
NN = (((1,), (0,)), ((), ()))
NT = (((1,), (1,)), ((), ()))


def shifted(block, distance):
    devices = lax.axis_size("blk")
    return lax.ppermute(block, "blk", [(i, (i + distance) % devices) for i in range(devices)])


def planes(x):
    one = x.astype(bf16)
    rest = x - one.astype(f32)
    two = rest.astype(bf16)
    return one, two, (rest - two.astype(f32)).astype(bf16)


def dot(a, b, dims=NN):
    return lax.dot_general(a, b, dims, preferred_element_type=f32)


def product(small, large):
    rows = small[0].shape[0]
    a = dot(jnp.concatenate(small, axis=0), large[0])
    b = dot(jnp.concatenate(small[:2], axis=0), large[1])
    c = dot(small[0], large[2])
    return a[:rows] + ((a[rows : 2 * rows] + b[:rows]) + (a[2 * rows :] + b[rows:] + c))


def tiles(extent, tile):
    return [(at, min(tile, extent - at)) for at in range(0, extent, tile)]


def orthonormal_rows(m):
    rank = m.shape[0]
    g = lax.dot_general(m, m, NT, precision=HIGH, preferred_element_type=f32)
    row = lax.broadcasted_iota(jnp.int32, (rank, 1), 0)
    scale = jnp.ones((rank, 1), f32)
    for j in range(rank):
        pivot = g[j : j + 1, j : j + 1]
        factor = jnp.where(row > j, g[:, j : j + 1] * (1.0 / pivot), 0.0)
        scale = jnp.where(row == j, lax.rsqrt(pivot), scale)
        m = m - factor * m[j : j + 1]
        g = g - factor * g[j : j + 1]
    return m * scale


def summed(parts_ref):
    total = parts_ref[0]
    for k in range(1, parts_ref.shape[0]):
        total = total + parts_ref[k]
    return total


def times(factor_ref, own_ref, skip):
    total = jnp.zeros((factor_ref.shape[0], own_ref.shape[1]), f32)
    for at, size in tiles(own_ref.shape[0], 256):
        total = total + product(planes(factor_ref[:, pl.ds(skip + at, size)]), planes(own_ref[pl.ds(at, size)]))
    return total


def message_kernel(start_ref, own_ref, out_ref):
    width = own_ref.shape[1]
    out_ref[:, pl.ds(width, start_ref.shape[1])] = start_ref[...]
    out_ref[:, pl.ds(0, width)] = times(start_ref, own_ref, 0)


def rows_kernel(left_ref, own_ref, out_ref):
    width = own_ref.shape[1]
    rows = left_ref[:, pl.ds(0, width)] - times(left_ref, own_ref, width)
    for k in range(out_ref.shape[0]):
        out_ref[k] = rows


def basis_kernel(parts_ref, out_ref):
    out_ref[...] = orthonormal_rows(summed(parts_ref))


def right_side(basis):
    rank, width = basis.shape
    zero = jnp.zeros((rank, width), f32)
    p = [x.astype(f32) for x in planes(basis)]
    sides = []
    for kept in (3, 2, 1):
        groups = []
        for k in range(4):
            groups += [p[k] if k < kept else zero, zero]
        sides.append(jnp.transpose(jnp.concatenate(groups, axis=0)).astype(bf16))
    return jnp.concatenate(sides, axis=0)


def columns(difference, right, rank):
    groups = jnp.transpose(dot(jnp.concatenate(difference, axis=1), right))
    return groups[:rank] + (groups[2 * rank : 3 * rank] + groups[4 * rank : 5 * rank])


def power_kernel(basis_ref, own_ref, left_ref, out_ref):
    rank = basis_ref.shape[0]
    right = right_side(basis_ref[...])
    total = jnp.zeros(basis_ref.shape, f32)
    for at, size in tiles(own_ref.shape[0], 640):
        part = pl.ds(at, size)
        difference = planes(left_ref[part] - own_ref[part])
        total = total + product(planes(columns(difference, right, rank)), difference)
    for k in range(out_ref.shape[0]):
        out_ref[k] = total


def factor_kernel(parts_ref, own_ref, left_ref, out_ref):
    basis = orthonormal_rows(summed(parts_ref))
    rank, width = basis.shape
    right = right_side(basis)
    out_ref[:, pl.ds(0, width)] = basis
    for at, size in tiles(own_ref.shape[0], 640):
        part = pl.ds(at, size)
        difference = planes(left_ref[part] - own_ref[part])
        out_ref[:, pl.ds(width + at, size)] = columns(difference, right, rank)


def change_side(basis):
    b = [x.astype(f32) for x in planes(basis)]
    zero = jnp.zeros_like(b[0])
    return jnp.concatenate([b[0], b[1], b[2], b[0], b[1], b[0], zero, zero], axis=0).astype(bf16)


def change(cols, side):
    c = [x.astype(f32) for x in planes(cols)]
    zero = jnp.zeros_like(cols)
    left = jnp.concatenate([c[0], c[0], c[0], c[1], c[1], c[2], zero, zero], axis=0)
    return dot(jnp.transpose(left).astype(bf16), side)


def half_kernel(message_ref, own_ref, out_ref):
    width = own_ref.shape[1]
    side = change_side(step_size * message_ref[:, pl.ds(0, width)])
    for at, size in tiles(own_ref.shape[0], 640):
        part = pl.ds(at, size)
        out_ref[part] = own_ref[part] + change(message_ref[:, pl.ds(width + at, size)], side)


def final_kernel(message_ref, half_ref, new_ref, cols_ref, held, sems):
    width = half_ref.shape[1]
    side = change_side(-step_size * message_ref[:, pl.ds(0, width)])
    copies = []
    for k, (at, size) in enumerate(tiles(half_ref.shape[0], 640)):
        part = pl.ds(at, size)
        cols = message_ref[:, pl.ds(width + at, size)]
        cols_ref[:, part] = cols
        held[part] = half_ref[part] + change(cols, side)
        copy = pltpu.make_async_copy(held.at[part], new_ref.at[part], sems.at[k])
        copy.start()
        copies.append(copy)
    for copy in copies:
        copy.wait()


def call(kernel, name, out_shape, out_specs, cost_us, scratch=(), mib=16):
    return lambda *args: pl.pallas_call(
        kernel,
        out_shape=out_shape,
        in_specs=[VMEM] * len(args),
        out_specs=out_specs,
        scratch_shapes=scratch,
        compiler_params=pltpu.CompilerParams(vmem_limit_bytes=mib * 2**20),
        cost_estimate=pl.CostEstimate(flops=int(cost_us * 1.15e9), bytes_accessed=0, transcendentals=0),
        name=name,
    )(*args)


def gathered(copies):
    return lax.all_to_all(copies, "tensor", 0, 0, tiled=True)


COST = dict(message=2, rows=8, basis=14, power=3, factor=3, half=3, final=3)


def shards(weights, warm_q):
    own = weights.T
    start = warm_q[0].T
    rank, extent = start.shape
    width = own.shape[1]
    ranks = lax.axis_size("tensor")
    shape = lambda *dims: jax.ShapeDtypeStruct(dims, f32)
    whole = shape(rank, width + extent)
    copies = shape(ranks, rank, width)

    message = call(message_kernel, "message", whole, VMEM, COST["message"])(start, own)
    sent, message = lax.optimization_barrier((own, message))
    left = shifted(message, 1)
    left_own = shifted(sent, 1)
    rows = call(rows_kernel, "rows", copies, VMEM, COST["rows"])(left, own)
    basis = call(basis_kernel, "basis", shape(rank, width), VMEM, COST["basis"], mib=4)(gathered(rows))
    power = call(power_kernel, "power", copies, VMEM, COST["power"])(basis, own, left_own)
    factor = call(factor_kernel, "factor", whole, VMEM, COST["factor"])(gathered(power), own, left_own)
    right = shifted(factor, -1)
    half = call(half_kernel, "half", shape(extent, width), VMEM, COST["half"])(factor, own)
    new, cols = call(
        final_kernel,
        "final",
        (shape(extent, width), shape(rank, extent)),
        (HBM, VMEM),
        COST["final"],
        scratch=[pltpu.VMEM((extent, width), f32), pltpu.SemaphoreType.DMA((len(tiles(extent, 640)),))],
    )(right, half)
    return new.T, cols.T[None]


def solution(mesh):
    in_specs = (P("blk", "tensor"), P("blk", "tensor", None))
    out_specs = (P("blk", "tensor"), P("blk", "tensor", None))
    return jax.shard_map(shards, mesh=mesh, in_specs=in_specs, out_specs=out_specs, check_vma=False)
```

```python
import functools

import jax
import jax.numpy as jnp
from jax import lax
from jax.experimental import pallas as pl
from jax.experimental.pallas import tpu as pltpu
from jax.sharding import PartitionSpec as P

HIGH = lax.Precision.HIGHEST
f32 = jnp.float32
bf16 = jnp.bfloat16
step_size = 0.5
VMEM = pl.BlockSpec(memory_space=pltpu.VMEM)
HBM = pl.BlockSpec(memory_space=pltpu.HBM)
NN = (((1,), (0,)), ((), ()))
NT = (((1,), (1,)), ((), ()))


def shifted(block, distance):
    devices = lax.axis_size("blk")
    return lax.ppermute(block, "blk", [(i, (i + distance) % devices) for i in range(devices)])


def planes(x):
    one = x.astype(bf16)
    rest = x - one.astype(f32)
    two = rest.astype(bf16)
    return one, two, (rest - two.astype(f32)).astype(bf16)


def dot(a, b, dims=NN):
    return lax.dot_general(a, b, dims, preferred_element_type=f32)


def product(small, large):
    rows = small[0].shape[0]
    a = dot(jnp.concatenate(small, axis=0), large[0])
    b = dot(jnp.concatenate(small[:2], axis=0), large[1])
    c = dot(small[0], large[2])
    return a[:rows] + ((a[rows : 2 * rows] + b[:rows]) + (a[2 * rows :] + b[rows:] + c))


def tiles(extent, tile):
    out, at = [], 0
    while at < extent:
        size = extent - at if extent - at <= tile + 128 else tile
        out.append((at, size))
        at += size
    return out


def orthonormal_rows(m):
    rank = m.shape[0]
    g = lax.dot_general(m, m, NT, precision=HIGH, preferred_element_type=f32)
    row = lax.broadcasted_iota(jnp.int32, (rank, 1), 0)
    scale = jnp.ones((rank, 1), f32)
    for j in range(rank):
        pivot = g[j : j + 1, j : j + 1]
        factor = jnp.where(row > j, g[:, j : j + 1] * (1.0 / pivot), 0.0)
        scale = jnp.where(row == j, lax.rsqrt(pivot), scale)
        m = m - factor * m[j : j + 1]
        g = g - factor * g[j : j + 1]
    return m * scale


def summed(parts_ref):
    total = parts_ref[0]
    for k in range(1, parts_ref.shape[0]):
        total = total + parts_ref[k]
    return total


def message_kernel(start_ref, own_ref, out_ref, *rest):
    *own_refs, sems = rest
    rank, extent = start_ref.shape
    width = own_ref.shape[1]
    copies, at = [], 0
    for ref in own_refs:
        for inner, size in tiles(ref.shape[0], 512):
            copies.append((at, size, ref.at[pl.ds(inner, size)]))
            at += size
    copies = [
        (at, size, ref, pltpu.make_async_copy(own_ref.at[pl.ds(at, size)], ref, sems.at[k]))
        for k, (at, size, ref) in enumerate(copies)
    ]
    factor = out_ref.at[:, pl.ds(width, extent)]
    fetch = pltpu.make_async_copy(start_ref, factor, sems.at[len(copies)])
    fetch.start()
    for *_, copy in copies:
        copy.start()
    fetch.wait()
    total = jnp.zeros((rank, width), f32)
    for at, size, ref, copy in copies:
        copy.wait()
        total = total + product(planes(factor[:, pl.ds(at, size)]), planes(ref[...]))
    out_ref[:, pl.ds(0, width)] = total


def pieces(refs, tile):
    at = 0
    for k, ref in enumerate(refs):
        for inner, size in tiles(ref.shape[0], tile):
            yield at + inner, size, pl.ds(inner, size), k
        at += ref.shape[0]


def rows_kernel(left_ref, *rest):
    *own_refs, out_ref = rest
    rank, width = out_ref.shape[1:]
    rows = left_ref[:, pl.ds(0, width)]
    for at, size, part, k in pieces(own_refs, 512):
        rows = rows - product(planes(left_ref[:, pl.ds(width + at, size)]), planes(own_refs[k][part]))
    for k in range(out_ref.shape[0]):
        out_ref[k] = rows


def right_side(basis):
    rank, width = basis.shape
    zero = jnp.zeros((rank, width), f32)
    p = [x.astype(f32) for x in planes(basis)]
    sides = []
    for kept in (3, 2, 1):
        groups = []
        for k in range(4):
            groups += [p[k] if k < kept else zero, zero]
        sides.append(jnp.transpose(jnp.concatenate(groups, axis=0)).astype(bf16))
    return jnp.concatenate(sides, axis=0)


def columns(difference, right, rank):
    groups = jnp.transpose(dot(jnp.concatenate(difference, axis=1), right))
    return groups[:rank] + (groups[2 * rank : 3 * rank] + groups[4 * rank : 5 * rank])


def powered(total, basis, own_ref, left_ref):
    rank = basis.shape[0]
    right = right_side(basis)
    for _, size, part, _ in pieces([own_ref], 768):
        difference = planes(left_ref[part] - own_ref[part])
        total = total + product(planes(columns(difference, right, rank)), difference)
    return total


def basis_kernel(mine_ref, other_ref, own_ref, left_ref, basis_ref, total_ref):
    basis = orthonormal_rows(mine_ref[...] + other_ref[...])
    basis_ref[...] = basis
    total_ref[...] = powered(jnp.zeros(basis.shape, f32), basis, own_ref, left_ref)


def power_kernel(basis_ref, total_ref, own_ref, left_ref, out_ref):
    total = powered(total_ref[...], basis_ref[...], own_ref, left_ref)
    for k in range(out_ref.shape[0]):
        out_ref[k] = total


def factor_kernel(parts_ref, *rest):
    *both, out_ref = rest
    own_refs, left_refs = both[: len(both) // 2], both[len(both) // 2 :]
    basis = orthonormal_rows(summed(parts_ref))
    rank, width = basis.shape
    right = right_side(basis)
    out_ref[:, pl.ds(0, width)] = basis
    for at, size, part, k in pieces(own_refs, 768):
        difference = planes(left_refs[k][part] - own_refs[k][part])
        out_ref[:, pl.ds(width + at, size)] = columns(difference, right, rank)


def change_side(basis):
    b = [x.astype(f32) for x in planes(basis)]
    zero = jnp.zeros_like(b[0])
    return jnp.concatenate([b[0], b[1], b[2], b[0], b[1], b[0], zero, zero], axis=0).astype(bf16)


def change(cols, side):
    c = [x.astype(f32) for x in planes(cols)]
    zero = jnp.zeros_like(cols)
    left = jnp.concatenate([c[0], c[0], c[0], c[1], c[1], c[2], zero, zero], axis=0)
    return dot(jnp.transpose(left).astype(bf16), side)


def half_kernel(message_ref, *rest):
    *own_refs, out_ref = rest
    width = out_ref.shape[1]
    side = change_side(step_size * message_ref[:, pl.ds(0, width)])
    for at, size, part, k in pieces(own_refs, 768):
        out_ref[pl.ds(at, size)] = own_refs[k][part] + change(message_ref[:, pl.ds(width + at, size)], side)


def final_kernel(message_ref, half_ref, new_ref, cols_ref, held, sems):
    width = half_ref.shape[1]
    side = change_side(-step_size * message_ref[:, pl.ds(0, width)])
    copies = []
    for k, (at, size) in enumerate(tiles(half_ref.shape[0], 768)):
        part = pl.ds(at, size)
        cols = message_ref[:, pl.ds(width + at, size)]
        cols_ref[:, part] = cols
        held[part] = half_ref[part] + change(cols, side)
        copy = pltpu.make_async_copy(held.at[part], new_ref.at[part], sems.at[k])
        copy.start()
        copies.append(copy)
    for copy in copies:
        copy.wait()


def call(kernel, name, out_shape, out_specs, cost_us, in_specs=None, scratch=(), mib=16):
    return lambda *args: pl.pallas_call(
        kernel,
        out_shape=out_shape,
        in_specs=in_specs or [VMEM] * len(args),
        out_specs=out_specs,
        scratch_shapes=scratch,
        compiler_params=pltpu.CompilerParams(vmem_limit_bytes=mib * 2**20),
        cost_estimate=pl.CostEstimate(flops=int(cost_us * 1.15e9), bytes_accessed=0, transcendentals=0),
        name=name,
    )(*args)


COST = dict(message=2, rows=20, basis=14, power=3, factor=3, half=3, final=3)
PARTS = (1536, 832)


def shards(weights, warm_q):
    own = weights.T
    start = warm_q[0].T
    rank, extent = start.shape
    width = own.shape[1]
    ranks = lax.axis_size("tensor")
    shape = lambda *dims: jax.ShapeDtypeStruct(dims, f32)
    whole = shape(rank, width + extent)
    rows_shape = shape(rank, width)

    message, *own = call(
        message_kernel,
        "message",
        (whole, *(shape(rows, width) for rows in PARTS)),
        (VMEM,) * 3,
        COST["message"],
        in_specs=[HBM, HBM],
        scratch=[pltpu.SemaphoreType.DMA((1 + sum(len(tiles(rows, 512)) for rows in PARTS),))],
        mib=60,
    )(start, own)
    left = shifted(message, 1)
    left_first = shifted(own[0], 1)
    copies = call(rows_kernel, "rows", shape(ranks // 2, rank, width), VMEM, COST["rows"])(left, *own)
    along_y = [[2 * y + x for y in range(ranks // 2)] for x in range(2)]
    rows = jnp.sum(lax.all_to_all(copies, "tensor", 0, 0, axis_index_groups=along_y, tiled=True), axis=0)
    other = lax.ppermute(rows, "tensor", [(t, t ^ 1) for t in range(ranks)])
    sent, rows = lax.optimization_barrier((own[1], rows))
    left_second = shifted(sent, 1)
    basis, total = call(basis_kernel, "basis", (rows_shape, rows_shape), (VMEM, VMEM), COST["basis"])(
        rows, other, own[0], left_first
    )
    copies = call(power_kernel, "power", shape(ranks, rank, width), VMEM, COST["power"])(
        basis, total, own[1], left_second
    )
    parts = lax.all_to_all(copies, "tensor", 0, 0, tiled=True)
    factor = call(factor_kernel, "factor", whole, VMEM, COST["factor"])(parts, *own, left_first, left_second)
    right = shifted(factor, -1)
    half = call(half_kernel, "half", shape(extent, width), VMEM, COST["half"])(factor, *own)
    new, cols = call(
        final_kernel,
        "final",
        (shape(extent, width), shape(rank, extent)),
        (HBM, VMEM),
        COST["final"],
        scratch=[pltpu.VMEM((extent, width), f32), pltpu.SemaphoreType.DMA((len(tiles(extent, 768)),))],
    )(right, half)
    return new.T, cols.T[None]


def solution(mesh):
    in_specs = (P("blk", "tensor"), P("blk", "tensor", None))
    out_specs = (P("blk", "tensor"), P("blk", "tensor", None))
    return jax.shard_map(shards, mesh=mesh, in_specs=in_specs, out_specs=out_specs, check_vma=False)
```

```python
import functools

import jax
import jax.numpy as jnp
from jax import lax
from jax.experimental import pallas as pl
from jax.experimental.pallas import tpu as pltpu
from jax.sharding import PartitionSpec as P

HIGH = lax.Precision.HIGHEST
f32 = jnp.float32
bf16 = jnp.bfloat16
step_size = 0.5
VMEM = pl.BlockSpec(memory_space=pltpu.VMEM)
HBM = pl.BlockSpec(memory_space=pltpu.HBM)
NN = (((1,), (0,)), ((), ()))
NT = (((1,), (1,)), ((), ()))


def shifted(block, distance):
    devices = lax.axis_size("blk")
    return lax.ppermute(block, "blk", [(i, (i + distance) % devices) for i in range(devices)])


def planes(x):
    one = x.astype(bf16)
    rest = x - one.astype(f32)
    two = rest.astype(bf16)
    return one, two, (rest - two.astype(f32)).astype(bf16)


def dot(a, b, dims=NN):
    return lax.dot_general(a, b, dims, preferred_element_type=f32)


def product(small, large):
    rows = small[0].shape[0]
    a = dot(jnp.concatenate(small, axis=0), large[0])
    b = dot(jnp.concatenate(small[:2], axis=0), large[1])
    c = dot(small[0], large[2])
    return a[:rows] + ((a[rows : 2 * rows] + b[:rows]) + (a[2 * rows :] + b[rows:] + c))


def tiles(extent, tile):
    out, at = [], 0
    while at < extent:
        size = extent - at if extent - at <= tile + 128 else tile
        out.append((at, size))
        at += size
    return out


def orthonormal_rows(m):
    rank = m.shape[0]
    g = lax.dot_general(m, m, NT, precision=HIGH, preferred_element_type=f32)
    row = lax.broadcasted_iota(jnp.int32, (rank, 1), 0)
    scale = jnp.ones((rank, 1), f32)
    for j in range(rank):
        pivot = g[j : j + 1, j : j + 1]
        factor = jnp.where(row > j, g[:, j : j + 1] * (1.0 / pivot), 0.0)
        scale = jnp.where(row == j, lax.rsqrt(pivot), scale)
        m = m - factor * m[j : j + 1]
        g = g - factor * g[j : j + 1]
    return m * scale


def summed(parts_ref):
    total = parts_ref[0]
    for k in range(1, parts_ref.shape[0]):
        total = total + parts_ref[k]
    return total


def message_kernel(start_ref, own_ref, out_ref, *rest):
    *own_refs, sems = rest
    rank, extent = start_ref.shape
    width = own_ref.shape[1]
    copies, at = [], 0
    for ref in own_refs:
        for inner, size in tiles(ref.shape[0], 512):
            copies.append((at, size, ref.at[pl.ds(inner, size)]))
            at += size
    copies = [
        (at, size, ref, pltpu.make_async_copy(own_ref.at[pl.ds(at, size)], ref, sems.at[k]))
        for k, (at, size, ref) in enumerate(copies)
    ]
    factor = out_ref.at[:, pl.ds(width, extent)]
    fetch = pltpu.make_async_copy(start_ref, factor, sems.at[len(copies)])
    fetch.start()
    for *_, copy in copies:
        copy.start()
    fetch.wait()
    total = jnp.zeros((rank, width), f32)
    for at, size, ref, copy in copies:
        copy.wait()
        total = total + product(planes(factor[:, pl.ds(at, size)]), planes(ref[...]))
    out_ref[:, pl.ds(0, width)] = total


def pieces(refs, tile):
    at = 0
    for k, ref in enumerate(refs):
        for inner, size in tiles(ref.shape[0], tile):
            yield at + inner, size, pl.ds(inner, size), k
        at += ref.shape[0]


def rows_kernel(left_ref, *rest):
    *own_refs, out_ref = rest
    rank, width = out_ref.shape
    rows = left_ref[:, pl.ds(0, width)]
    for at, size, part, k in pieces(own_refs, 512):
        rows = rows - product(planes(left_ref[:, pl.ds(width + at, size)]), planes(own_refs[k][part]))
    out_ref[...] = rows


def right_side(basis):
    rank, width = basis.shape
    zero = jnp.zeros((rank, width), f32)
    p = [x.astype(f32) for x in planes(basis)]
    sides = []
    for kept in (3, 2, 1):
        groups = []
        for k in range(4):
            groups += [p[k] if k < kept else zero, zero]
        sides.append(jnp.transpose(jnp.concatenate(groups, axis=0)).astype(bf16))
    return jnp.concatenate(sides, axis=0)


def columns(difference, right, rank):
    groups = jnp.transpose(dot(jnp.concatenate(difference, axis=1), right))
    return groups[:rank] + (groups[2 * rank : 3 * rank] + groups[4 * rank : 5 * rank])


def powered(total, basis, own_ref, left_ref):
    rank = basis.shape[0]
    right = right_side(basis)
    for _, size, part, _ in pieces([own_ref], 768):
        difference = planes(left_ref[part] - own_ref[part])
        total = total + product(planes(columns(difference, right, rank)), difference)
    return total


def basis_kernel(parts_ref, own_ref, left_ref, basis_ref, total_ref):
    basis = orthonormal_rows(summed(parts_ref))
    basis_ref[...] = basis
    total_ref[...] = powered(jnp.zeros(basis.shape, f32), basis, own_ref, left_ref)


def power_kernel(basis_ref, total_ref, own_ref, left_ref, out_ref):
    total = powered(total_ref[...], basis_ref[...], own_ref, left_ref)
    if len(out_ref.shape) == 2:
        out_ref[...] = total
    else:
        for k in range(out_ref.shape[0]):
            out_ref[k] = total


def factor_kernel(parts_ref, *rest):
    *both, out_ref = rest
    own_refs, left_refs = both[: len(both) // 2], both[len(both) // 2 :]
    basis = orthonormal_rows(summed(parts_ref))
    rank, width = basis.shape
    right = right_side(basis)
    out_ref[:, pl.ds(0, width)] = basis
    for at, size, part, k in pieces(own_refs, 768):
        difference = planes(left_refs[k][part] - own_refs[k][part])
        out_ref[:, pl.ds(width + at, size)] = columns(difference, right, rank)


def change_side(basis):
    b = [x.astype(f32) for x in planes(basis)]
    zero = jnp.zeros_like(b[0])
    return jnp.concatenate([b[0], b[1], b[2], b[0], b[1], b[0], zero, zero], axis=0).astype(bf16)


def change(cols, side):
    c = [x.astype(f32) for x in planes(cols)]
    zero = jnp.zeros_like(cols)
    left = jnp.concatenate([c[0], c[0], c[0], c[1], c[1], c[2], zero, zero], axis=0)
    return dot(jnp.transpose(left).astype(bf16), side)


def half_kernel(message_ref, *rest):
    *own_refs, out_ref = rest
    width = out_ref.shape[1]
    side = change_side(step_size * message_ref[:, pl.ds(0, width)])
    for at, size, part, k in pieces(own_refs, 768):
        out_ref[pl.ds(at, size)] = own_refs[k][part] + change(message_ref[:, pl.ds(width + at, size)], side)


def final_kernel(message_ref, half_ref, new_ref, cols_ref, held, sems):
    width = half_ref.shape[1]
    side = change_side(-step_size * message_ref[:, pl.ds(0, width)])
    copies = []
    for k, (at, size) in enumerate(tiles(half_ref.shape[0], 768)):
        part = pl.ds(at, size)
        cols = message_ref[:, pl.ds(width + at, size)]
        cols_ref[:, part] = cols
        held[part] = half_ref[part] + change(cols, side)
        copy = pltpu.make_async_copy(held.at[part], new_ref.at[part], sems.at[k])
        copy.start()
        copies.append(copy)
    for copy in copies:
        copy.wait()


def call(kernel, name, out_shape, out_specs, cost_us, in_specs=None, scratch=(), mib=16):
    return lambda *args: pl.pallas_call(
        kernel,
        out_shape=out_shape,
        in_specs=in_specs or [VMEM] * len(args),
        out_specs=out_specs,
        scratch_shapes=scratch,
        compiler_params=pltpu.CompilerParams(vmem_limit_bytes=mib * 2**20),
        cost_estimate=pl.CostEstimate(flops=int(cost_us * 1.15e9), bytes_accessed=0, transcendentals=0),
        name=name,
    )(*args)


COST = dict(message=2, rows=20, basis=10.45, power=3, factor=3, half=3, final=3)
PARTS = (512, 1152, 704)


def shards(weights, warm_q):
    own = weights.T
    start = warm_q[0].T
    rank, extent = start.shape
    width = own.shape[1]
    ranks = lax.axis_size("tensor")
    shape = lambda *dims: jax.ShapeDtypeStruct(dims, f32)
    whole = shape(rank, width + extent)
    rows_shape = shape(rank, width)

    message, *own = call(
        message_kernel,
        "message",
        (whole, *(shape(rows, width) for rows in PARTS)),
        (VMEM,) * (1 + len(PARTS)),
        COST["message"],
        in_specs=[HBM, HBM],
        scratch=[pltpu.SemaphoreType.DMA((1 + sum(len(tiles(rows, 512)) for rows in PARTS),))],
        mib=50,
    )(start, own)
    left = shifted(message, 1)
    lefts = [shifted(own[0], 1)]
    rows = call(rows_kernel, "rows", rows_shape, VMEM, COST["rows"])(left, *own)
    other = lax.ppermute(rows, "tensor", [(t, t ^ 1) for t in range(ranks)])
    *sent, rows = lax.optimization_barrier((*own[1:], rows))
    lefts += [shifted(piece, 1) for piece in sent]
    along_y = [[2 * y + x for y in range(ranks // 2)] for x in range(2)]
    copies = jnp.broadcast_to((rows + other)[None], (ranks // 2, rank, width))
    parts = lax.all_to_all(copies, "tensor", 0, 0, axis_index_groups=along_y, tiled=True)
    basis, total = call(basis_kernel, "basis", (rows_shape, rows_shape), (VMEM, VMEM), COST["basis"])(
        parts, own[0], lefts[0]
    )
    for piece, near in zip(own[1:-1], lefts[1:-1]):
        total = call(power_kernel, "power", rows_shape, VMEM, COST["power"])(basis, total, piece, near)
    copies = call(power_kernel, "power", shape(ranks, rank, width), VMEM, COST["power"])(
        basis, total, own[-1], lefts[-1]
    )
    parts = lax.all_to_all(copies, "tensor", 0, 0, tiled=True)
    factor = call(factor_kernel, "factor", whole, VMEM, COST["factor"])(parts, *own, *lefts)
    right = shifted(factor, -1)
    half = call(half_kernel, "half", shape(extent, width), VMEM, COST["half"])(factor, *own)
    new, cols = call(
        final_kernel,
        "final",
        (shape(extent, width), shape(rank, extent)),
        (HBM, VMEM),
        COST["final"],
        scratch=[pltpu.VMEM((extent, width), f32), pltpu.SemaphoreType.DMA((len(tiles(extent, 768)),))],
    )(right, half)
    return new.T, cols.T[None]


def solution(mesh):
    in_specs = (P("blk", "tensor"), P("blk", "tensor", None))
    out_specs = (P("blk", "tensor"), P("blk", "tensor", None))
    return jax.shard_map(shards, mesh=mesh, in_specs=in_specs, out_specs=out_specs, check_vma=False)
```

```python
import functools

import jax
import jax.numpy as jnp
from jax import lax
from jax.experimental import pallas as pl
from jax.experimental.pallas import tpu as pltpu
from jax.sharding import PartitionSpec as P

HIGH = lax.Precision.HIGHEST
f32 = jnp.float32
bf16 = jnp.bfloat16
step_size = 0.5
VMEM = pl.BlockSpec(memory_space=pltpu.VMEM)
HBM = pl.BlockSpec(memory_space=pltpu.HBM)
NN = (((1,), (0,)), ((), ()))
NT = (((1,), (1,)), ((), ()))


def shifted(block, distance):
    devices = lax.axis_size("blk")
    return lax.ppermute(block, "blk", [(i, (i + distance) % devices) for i in range(devices)])


def planes(x):
    one = x.astype(bf16)
    rest = x - one.astype(f32)
    two = rest.astype(bf16)
    return one, two, (rest - two.astype(f32)).astype(bf16)


def dot(a, b, dims=NN):
    return lax.dot_general(a, b, dims, preferred_element_type=f32)


def product(small, large):
    rows = small[0].shape[0]
    a = dot(jnp.concatenate(small, axis=0), large[0])
    b = dot(jnp.concatenate(small[:2], axis=0), large[1])
    c = dot(small[0], large[2])
    return a[:rows] + ((a[rows : 2 * rows] + b[:rows]) + (a[2 * rows :] + b[rows:] + c))


def tiles(extent, tile):
    out, at = [], 0
    while at < extent:
        size = extent - at if extent - at <= tile + 128 else tile
        out.append((at, size))
        at += size
    return out


def orthonormal_rows(m):
    rank = m.shape[0]
    g = lax.dot_general(m, m, NT, precision=HIGH, preferred_element_type=f32)
    row = lax.broadcasted_iota(jnp.int32, (rank, 1), 0)
    scale = jnp.ones((rank, 1), f32)
    for j in range(rank):
        pivot = g[j : j + 1, j : j + 1]
        factor = jnp.where(row > j, g[:, j : j + 1] * (1.0 / pivot), 0.0)
        scale = jnp.where(row == j, lax.rsqrt(pivot), scale)
        m = m - factor * m[j : j + 1]
        g = g - factor * g[j : j + 1]
    return m * scale


def summed(parts_ref):
    total = parts_ref[0]
    for k in range(1, parts_ref.shape[0]):
        total = total + parts_ref[k]
    return total


def message_kernel(start_ref, own_ref, out_ref, held, sems):
    rank, extent = start_ref.shape
    width = own_ref.shape[1]
    factor = out_ref.at[:, pl.ds(width, extent)]
    fetch = pltpu.make_async_copy(start_ref, factor, sems.at[0])
    fetch.start()
    copies = []
    for k, (at, size) in enumerate(tiles(extent, 512)):
        part = pl.ds(at, size)
        copies.append((at, size, pltpu.make_async_copy(own_ref.at[part], held.at[part], sems.at[1 + k])))
        copies[-1][2].start()
    fetch.wait()
    total = jnp.zeros((rank, width), f32)
    for at, size, copy in copies:
        copy.wait()
        total = total + product(planes(factor[:, pl.ds(at, size)]), planes(held[pl.ds(at, size)]))
    out_ref[:, pl.ds(0, width)] = total


def rows_kernel(left_ref, own_ref, out_ref):
    width = own_ref.shape[1]
    rows = left_ref[:, pl.ds(0, width)]
    for at, size in tiles(own_ref.shape[0], 512):
        rows = rows - product(planes(left_ref[:, pl.ds(width + at, size)]), planes(own_ref[pl.ds(at, size)]))
    for k in range(out_ref.shape[0]):
        out_ref[k] = rows


def right_side(basis):
    rank, width = basis.shape
    zero = jnp.zeros((rank, width), f32)
    p = [x.astype(f32) for x in planes(basis)]
    sides = []
    for kept in (3, 2, 1):
        groups = []
        for k in range(4):
            groups += [p[k] if k < kept else zero, zero]
        sides.append(jnp.transpose(jnp.concatenate(groups, axis=0)).astype(bf16))
    return jnp.concatenate(sides, axis=0)


def columns(difference, right, rank):
    groups = jnp.transpose(dot(jnp.concatenate(difference, axis=1), right))
    return groups[:rank] + (groups[2 * rank : 3 * rank] + groups[4 * rank : 5 * rank])


def basis_kernel(mine_ref, other_ref, out_ref):
    out_ref[...] = orthonormal_rows(mine_ref[...] + other_ref[...])


def fetched(left_ref, held, sems):
    copies = []
    for k, (at, size) in enumerate(tiles(held.shape[0], 768)):
        part = pl.ds(at, size)
        copies.append((part, at, size, pltpu.make_async_copy(left_ref.at[part], held.at[part], sems.at[k])))
        copies[-1][3].start()
    return copies


def power_kernel(basis_ref, own_ref, left_ref, out_ref, held, sems):
    rank, width = basis_ref.shape
    copies = fetched(left_ref, held, sems)
    right = right_side(basis_ref[...])
    total = jnp.zeros((rank, width), f32)
    for part, _, _, copy in copies:
        copy.wait()
        difference = planes(held[part] - own_ref[part])
        total = total + product(planes(columns(difference, right, rank)), difference)
    for k in range(out_ref.shape[0]):
        out_ref[k] = total


def factor_kernel(parts_ref, own_ref, left_ref, out_ref, held, sems):
    copies = fetched(left_ref, held, sems)
    basis = orthonormal_rows(summed(parts_ref))
    rank, width = basis.shape
    right = right_side(basis)
    out_ref[:, pl.ds(0, width)] = basis
    for part, at, size, copy in copies:
        copy.wait()
        difference = planes(held[part] - own_ref[part])
        out_ref[:, pl.ds(width + at, size)] = columns(difference, right, rank)


def change_side(basis):
    b = [x.astype(f32) for x in planes(basis)]
    zero = jnp.zeros_like(b[0])
    return jnp.concatenate([b[0], b[1], b[2], b[0], b[1], b[0], zero, zero], axis=0).astype(bf16)


def change(cols, side):
    c = [x.astype(f32) for x in planes(cols)]
    zero = jnp.zeros_like(cols)
    left = jnp.concatenate([c[0], c[0], c[0], c[1], c[1], c[2], zero, zero], axis=0)
    return dot(jnp.transpose(left).astype(bf16), side)


def half_kernel(message_ref, own_ref, out_ref):
    width = own_ref.shape[1]
    side = change_side(step_size * message_ref[:, pl.ds(0, width)])
    for at, size in tiles(own_ref.shape[0], 768):
        part = pl.ds(at, size)
        out_ref[part] = own_ref[part] + change(message_ref[:, pl.ds(width + at, size)], side)


def final_kernel(message_ref, half_ref, new_ref, cols_ref, held, sems):
    extent, width = half_ref.shape
    copies = [pltpu.make_async_copy(message_ref.at[:, pl.ds(width, extent)], cols_ref, sems.at[0])]
    copies[0].start()
    side = change_side(-step_size * message_ref[:, pl.ds(0, width)])
    for k, (at, size) in enumerate(tiles(extent, 256)):
        part = pl.ds(at, size)
        held[part] = half_ref[part] + change(message_ref[:, pl.ds(width + at, size)], side)
        copies.append(pltpu.make_async_copy(held.at[part], new_ref.at[part], sems.at[1 + k]))
        copies[-1].start()
    for copy in copies:
        copy.wait()


def call(kernel, name, out_shape, out_specs, cost_us, in_specs=None, scratch=(), mib=16):
    return lambda *args: pl.pallas_call(
        kernel,
        out_shape=out_shape,
        in_specs=in_specs or [VMEM] * len(args),
        out_specs=out_specs,
        scratch_shapes=scratch,
        compiler_params=pltpu.CompilerParams(vmem_limit_bytes=mib * 2**20),
        cost_estimate=pl.CostEstimate(flops=int(cost_us * 1.15e9), bytes_accessed=0, transcendentals=0),
        name=name,
    )(*args)


COST = dict(message=2, rows=8, basis=14, power=3, factor=3, half=3, final=3)


def shards(weights, warm_q):
    own = weights.T
    start = warm_q[0].T
    rank, extent = start.shape
    width = own.shape[1]
    ranks = lax.axis_size("tensor")
    shape = lambda *dims: jax.ShapeDtypeStruct(dims, f32)
    whole = shape(rank, width + extent)
    held = pltpu.VMEM((extent, width), f32)
    sems = lambda tile: pltpu.SemaphoreType.DMA((1 + len(tiles(extent, tile)),))

    near = dict(in_specs=[VMEM, VMEM, HBM], scratch=[held, sems(768)])

    message = call(
        message_kernel,
        "message",
        whole,
        VMEM,
        COST["message"],
        in_specs=[HBM, HBM],
        scratch=[held, sems(512)],
        mib=60,
    )(start, own)
    left = shifted(message, 1)
    left_own = shifted(lax.optimization_barrier((own, message))[0], 1)
    copies = call(rows_kernel, "rows", shape(ranks // 2, rank, width), VMEM, COST["rows"])(left, own)
    along_y = [[2 * y + x for y in range(ranks // 2)] for x in range(2)]
    rows = jnp.sum(lax.all_to_all(copies, "tensor", 0, 0, axis_index_groups=along_y, tiled=True), axis=0)
    other = lax.ppermute(rows, "tensor", [(t, t ^ 1) for t in range(ranks)])
    basis = call(basis_kernel, "basis", shape(rank, width), VMEM, COST["basis"], mib=4)(rows, other)
    copies = call(power_kernel, "power", shape(ranks, rank, width), VMEM, COST["power"], **near)(basis, own, left_own)
    parts = lax.all_to_all(copies, "tensor", 0, 0, tiled=True)
    factor = call(factor_kernel, "factor", whole, VMEM, COST["factor"], **near)(parts, own, left_own)
    right = shifted(factor, -1)
    half = call(half_kernel, "half", shape(extent, width), VMEM, COST["half"])(factor, own)
    new, cols = call(
        final_kernel,
        "final",
        (shape(extent, width), shape(rank, extent)),
        (HBM, HBM),
        COST["final"],
        scratch=[held, sems(256)],
    )(right, half)
    return new.T, cols.T[None]


def solution(mesh):
    in_specs = (P("blk", "tensor"), P("blk", "tensor", None))
    out_specs = (P("blk", "tensor"), P("blk", "tensor", None))
    return jax.shard_map(shards, mesh=mesh, in_specs=in_specs, out_specs=out_specs, check_vma=False)
```

```python
import functools

import jax
import jax.numpy as jnp
from jax import lax
from jax.experimental import pallas as pl
from jax.experimental.pallas import tpu as pltpu
from jax.sharding import PartitionSpec as P

HIGH = lax.Precision.HIGHEST
f32 = jnp.float32
bf16 = jnp.bfloat16
step_size = 0.5
VMEM = pl.BlockSpec(memory_space=pltpu.VMEM)
HBM = pl.BlockSpec(memory_space=pltpu.HBM)
NN = (((1,), (0,)), ((), ()))
NT = (((1,), (1,)), ((), ()))


def shifted(block, distance):
    devices = lax.axis_size("blk")
    return lax.ppermute(block, "blk", [(i, (i + distance) % devices) for i in range(devices)])


def planes(x):
    one = x.astype(bf16)
    rest = x - one.astype(f32)
    two = rest.astype(bf16)
    return one, two, (rest - two.astype(f32)).astype(bf16)


def dot(a, b, dims=NN):
    return lax.dot_general(a, b, dims, preferred_element_type=f32)


def product(small, large):
    rows = small[0].shape[0]
    a = dot(jnp.concatenate(small, axis=0), large[0])
    b = dot(jnp.concatenate(small[:2], axis=0), large[1])
    c = dot(small[0], large[2])
    return a[:rows] + ((a[rows : 2 * rows] + b[:rows]) + (a[2 * rows :] + b[rows:] + c))


def tiles(extent, tile):
    out, at = [], 0
    while at < extent:
        size = extent - at if extent - at <= tile + 128 else tile
        out.append((at, size))
        at += size
    return out


def orthonormal_rows(m):
    rank = m.shape[0]
    g = lax.dot_general(m, m, NT, precision=HIGH, preferred_element_type=f32)
    row = lax.broadcasted_iota(jnp.int32, (rank, 1), 0)
    scale = jnp.ones((rank, 1), f32)
    for j in range(rank):
        pivot = g[j : j + 1, j : j + 1]
        factor = jnp.where(row > j, g[:, j : j + 1] * (1.0 / pivot), 0.0)
        scale = jnp.where(row == j, lax.rsqrt(pivot), scale)
        m = m - factor * m[j : j + 1]
        g = g - factor * g[j : j + 1]
    return m * scale


def summed(parts_ref):
    total = parts_ref[0]
    for k in range(1, parts_ref.shape[0]):
        total = total + parts_ref[k]
    return total


def message_kernel(start_ref, own_ref, out_ref, held, sems):
    rank, extent = start_ref.shape
    width = own_ref.shape[1]
    factor = out_ref.at[:, pl.ds(width, extent)]
    fetch = pltpu.make_async_copy(start_ref, factor, sems.at[0])
    fetch.start()
    copies = []
    for k, (at, size) in enumerate(tiles(extent, 512)):
        part = pl.ds(at, size)
        copies.append((at, size, pltpu.make_async_copy(own_ref.at[part], held.at[part], sems.at[1 + k])))
        copies[-1][2].start()
    fetch.wait()
    total = jnp.zeros((rank, width), f32)
    for at, size, copy in copies:
        copy.wait()
        total = total + product(planes(factor[:, pl.ds(at, size)]), planes(held[pl.ds(at, size)]))
    out_ref[:, pl.ds(0, width)] = total


def rows_kernel(left_ref, own_ref, out_ref):
    width = own_ref.shape[1]
    rows = left_ref[:, pl.ds(0, width)]
    for at, size in tiles(own_ref.shape[0], 512):
        rows = rows - product(planes(left_ref[:, pl.ds(width + at, size)]), planes(own_ref[pl.ds(at, size)]))
    for k in range(out_ref.shape[0]):
        out_ref[k] = rows


def right_side(basis):
    rank, width = basis.shape
    zero = jnp.zeros((rank, width), f32)
    p = [x.astype(f32) for x in planes(basis)]
    sides = []
    for kept in (3, 2, 1):
        groups = []
        for k in range(4):
            groups += [p[k] if k < kept else zero, zero]
        sides.append(jnp.transpose(jnp.concatenate(groups, axis=0)).astype(bf16))
    return jnp.concatenate(sides, axis=0)


def columns(difference, right, rank):
    groups = jnp.transpose(dot(jnp.concatenate(difference, axis=1), right))
    return groups[:rank] + (groups[2 * rank : 3 * rank] + groups[4 * rank : 5 * rank])


def powered(total, basis, own_ref, left_ref, first):
    rank = basis.shape[0]
    right = right_side(basis)
    for at, size in tiles(left_ref.shape[0], 768):
        difference = planes(left_ref[pl.ds(at, size)] - own_ref[pl.ds(first + at, size)])
        total = total + product(planes(columns(difference, right, rank)), difference)
    return total


def sum_kernel(parts_ref, out_ref):
    out_ref[...] = summed(parts_ref)


def basis_kernel(mine_ref, other_ref, own_ref, left_ref, basis_ref, total_ref):
    basis = orthonormal_rows(mine_ref[...] + other_ref[...])
    basis_ref[...] = basis
    total_ref[...] = powered(jnp.zeros(basis.shape, f32), basis, own_ref, left_ref, 0)


def power_kernel(basis_ref, total_ref, own_ref, left_ref, out_ref):
    first = own_ref.shape[0] - left_ref.shape[0]
    total = powered(total_ref[...], basis_ref[...], own_ref, left_ref, first)
    for k in range(out_ref.shape[0]):
        out_ref[k] = total


def factor_kernel(parts_ref, own_ref, *rest):
    *left_refs, out_ref = rest
    basis = orthonormal_rows(summed(parts_ref))
    rank, width = basis.shape
    right = right_side(basis)
    out_ref[:, pl.ds(0, width)] = basis
    first = 0
    for left_ref in left_refs:
        for at, size in tiles(left_ref.shape[0], 768):
            difference = planes(left_ref[pl.ds(at, size)] - own_ref[pl.ds(first + at, size)])
            out_ref[:, pl.ds(width + first + at, size)] = columns(difference, right, rank)
        first += left_ref.shape[0]


def change_side(basis):
    b = [x.astype(f32) for x in planes(basis)]
    zero = jnp.zeros_like(b[0])
    return jnp.concatenate([b[0], b[1], b[2], b[0], b[1], b[0], zero, zero], axis=0).astype(bf16)


def change(cols, side):
    c = [x.astype(f32) for x in planes(cols)]
    zero = jnp.zeros_like(cols)
    left = jnp.concatenate([c[0], c[0], c[0], c[1], c[1], c[2], zero, zero], axis=0)
    return dot(jnp.transpose(left).astype(bf16), side)


def half_kernel(message_ref, own_ref, out_ref):
    width = own_ref.shape[1]
    side = change_side(step_size * message_ref[:, pl.ds(0, width)])
    for at, size in tiles(own_ref.shape[0], 768):
        part = pl.ds(at, size)
        out_ref[part] = own_ref[part] + change(message_ref[:, pl.ds(width + at, size)], side)


def final_kernel(message_ref, half_ref, new_ref, cols_ref, held, sems):
    extent, width = half_ref.shape
    copies = [pltpu.make_async_copy(message_ref.at[:, pl.ds(width, extent)], cols_ref, sems.at[0])]
    copies[0].start()
    side = change_side(-step_size * message_ref[:, pl.ds(0, width)])
    for k, (at, size) in enumerate(tiles(extent, 256)):
        part = pl.ds(at, size)
        held[part] = half_ref[part] + change(message_ref[:, pl.ds(width + at, size)], side)
        copies.append(pltpu.make_async_copy(held.at[part], new_ref.at[part], sems.at[1 + k]))
        copies[-1].start()
    for copy in copies:
        copy.wait()


def call(kernel, name, out_shape, out_specs, cost_us, in_specs=None, scratch=(), mib=16):
    return lambda *args: pl.pallas_call(
        kernel,
        out_shape=out_shape,
        in_specs=in_specs or [VMEM] * len(args),
        out_specs=out_specs,
        scratch_shapes=scratch,
        compiler_params=pltpu.CompilerParams(vmem_limit_bytes=mib * 2**20),
        cost_estimate=pl.CostEstimate(flops=int(cost_us * 1.15e9), bytes_accessed=0, transcendentals=0),
        name=name,
    )(*args)


COST = dict(message=2, sum=1, rows=20, basis=14, power=3, factor=3, half=3, final=3)
FIRST = 1536


def shards(weights, warm_q):
    own = weights.T
    start = warm_q[0].T
    rank, extent = start.shape
    width = own.shape[1]
    ranks = lax.axis_size("tensor")
    shape = lambda *dims: jax.ShapeDtypeStruct(dims, f32)
    whole = shape(rank, width + extent)
    held = pltpu.VMEM((extent, width), f32)
    sems = lambda tile: pltpu.SemaphoreType.DMA((1 + len(tiles(extent, tile)),))

    message = call(
        message_kernel,
        "message",
        whole,
        VMEM,
        COST["message"],
        in_specs=[HBM, HBM],
        scratch=[held, sems(512)],
        mib=60,
    )(start, own)
    own, message = lax.optimization_barrier((own, message))
    left = shifted(message, 1)
    left_first = shifted(own[:FIRST], 1)
    copies = call(rows_kernel, "rows", shape(ranks // 2, rank, width), VMEM, COST["rows"])(left, own)
    along_y = [[2 * y + x for y in range(ranks // 2)] for x in range(2)]
    parts = lax.all_to_all(copies, "tensor", 0, 0, axis_index_groups=along_y, tiled=True)
    rows = call(sum_kernel, "sum", shape(rank, width), VMEM, COST["sum"], mib=4)(parts)
    other = lax.ppermute(rows, "tensor", [(t, t ^ 1) for t in range(ranks)])
    rest, rows = lax.optimization_barrier((own[FIRST:], rows))
    left_rest = shifted(rest, 1)
    both = (shape(rank, width),) * 2
    basis, total = call(basis_kernel, "basis", both, (VMEM, VMEM), COST["basis"])(rows, other, own, left_first)
    copies = call(power_kernel, "power", shape(ranks, rank, width), VMEM, COST["power"])(
        basis, total, own, left_rest
    )
    parts = lax.all_to_all(copies, "tensor", 0, 0, tiled=True)
    factor = call(factor_kernel, "factor", whole, VMEM, COST["factor"])(parts, own, left_first, left_rest)
    right = shifted(factor, -1)
    half = call(half_kernel, "half", shape(extent, width), VMEM, COST["half"])(factor, own)
    new, cols = call(
        final_kernel,
        "final",
        (shape(extent, width), shape(rank, extent)),
        (HBM, HBM),
        COST["final"],
        scratch=[held, sems(256)],
    )(right, half)
    return new.T, cols.T[None]


def solution(mesh):
    in_specs = (P("blk", "tensor"), P("blk", "tensor", None))
    out_specs = (P("blk", "tensor"), P("blk", "tensor", None))
    return jax.shard_map(shards, mesh=mesh, in_specs=in_specs, out_specs=out_specs, check_vma=False)
```

```python
import functools

import jax
import jax.numpy as jnp
from jax import lax
from jax.experimental import pallas as pl
from jax.experimental.pallas import tpu as pltpu
from jax.sharding import PartitionSpec as P

HIGH = lax.Precision.HIGHEST
f32 = jnp.float32
bf16 = jnp.bfloat16
step_size = 0.5
VMEM = pl.BlockSpec(memory_space=pltpu.VMEM)
HBM = pl.BlockSpec(memory_space=pltpu.HBM)
NN = (((1,), (0,)), ((), ()))
NT = (((1,), (1,)), ((), ()))


def shifted(block, distance):
    devices = lax.axis_size("blk")
    return lax.ppermute(block, "blk", [(i, (i + distance) % devices) for i in range(devices)])


def planes(x):
    one = x.astype(bf16)
    rest = x - one.astype(f32)
    two = rest.astype(bf16)
    return one, two, (rest - two.astype(f32)).astype(bf16)


def dot(a, b, dims=NN):
    return lax.dot_general(a, b, dims, preferred_element_type=f32)


def product(small, large):
    rows = small[0].shape[0]
    a = dot(jnp.concatenate(small, axis=0), large[0])
    b = dot(jnp.concatenate(small[:2], axis=0), large[1])
    c = dot(small[0], large[2])
    return a[:rows] + ((a[rows : 2 * rows] + b[:rows]) + (a[2 * rows :] + b[rows:] + c))


def tiles(extent, tile):
    out, at = [], 0
    while at < extent:
        size = extent - at if extent - at <= tile + 128 else tile
        out.append((at, size))
        at += size
    return out


def orthonormal_rows(m):
    rank = m.shape[0]
    g = lax.dot_general(m, m, NT, precision=HIGH, preferred_element_type=f32)
    row = lax.broadcasted_iota(jnp.int32, (rank, 1), 0)
    scale = jnp.ones((rank, 1), f32)
    for j in range(rank):
        pivot = g[j : j + 1, j : j + 1]
        factor = jnp.where(row > j, g[:, j : j + 1] * (1.0 / pivot), 0.0)
        scale = jnp.where(row == j, lax.rsqrt(pivot), scale)
        m = m - factor * m[j : j + 1]
        g = g - factor * g[j : j + 1]
    return m * scale


def summed(parts_ref):
    total = parts_ref[0]
    for k in range(1, parts_ref.shape[0]):
        total = total + parts_ref[k]
    return total


def message_kernel(start_ref, own_ref, out_ref, held, sems):
    rank, extent = start_ref.shape
    width = own_ref.shape[1]
    factor = out_ref.at[:, pl.ds(width, extent)]
    fetch = pltpu.make_async_copy(start_ref, factor, sems.at[0])
    fetch.start()
    copies = []
    for k, (at, size) in enumerate(tiles(extent, 512)):
        part = pl.ds(at, size)
        copies.append((at, size, pltpu.make_async_copy(own_ref.at[part], held.at[part], sems.at[1 + k])))
        copies[-1][2].start()
    fetch.wait()
    total = jnp.zeros((rank, width), f32)
    for at, size, copy in copies:
        copy.wait()
        total = total + product(planes(factor[:, pl.ds(at, size)]), planes(held[pl.ds(at, size)]))
    out_ref[:, pl.ds(0, width)] = total


def rows_kernel(left_ref, own_ref, out_ref):
    width = own_ref.shape[1]
    rows = left_ref[:, pl.ds(0, width)]
    for at, size in tiles(own_ref.shape[0], 512):
        rows = rows - product(planes(left_ref[:, pl.ds(width + at, size)]), planes(own_ref[pl.ds(at, size)]))
    for k in range(out_ref.shape[0]):
        out_ref[k] = rows


def right_side(basis):
    rank, width = basis.shape
    zero = jnp.zeros((rank, width), f32)
    p = [x.astype(f32) for x in planes(basis)]
    sides = []
    for kept in (3, 2, 1):
        groups = []
        for k in range(4):
            groups += [p[k] if k < kept else zero, zero]
        sides.append(jnp.transpose(jnp.concatenate(groups, axis=0)).astype(bf16))
    return jnp.concatenate(sides, axis=0)


def columns(difference, right, rank):
    groups = jnp.transpose(dot(jnp.concatenate(difference, axis=1), right))
    return groups[:rank] + (groups[2 * rank : 3 * rank] + groups[4 * rank : 5 * rank])


def powered(total, basis, own_ref, left_ref, first):
    rank = basis.shape[0]
    right = right_side(basis)
    for at, size in tiles(left_ref.shape[0], 896):
        difference = planes(left_ref[pl.ds(at, size)] - own_ref[pl.ds(first + at, size)])
        total = total + product(planes(columns(difference, right, rank)), difference)
    return total


def sum_kernel(parts_ref, out_ref):
    out_ref[...] = summed(parts_ref)


def basis_kernel(mine_ref, other_ref, own_ref, left_ref, basis_ref, total_ref):
    basis = orthonormal_rows(mine_ref[...] + other_ref[...])
    basis_ref[...] = basis
    total_ref[...] = powered(jnp.zeros(basis.shape, f32), basis, own_ref, left_ref, 0)


def power_kernel(basis_ref, total_ref, own_ref, left_ref, out_ref):
    first = own_ref.shape[0] - left_ref.shape[0]
    total = powered(total_ref[...], basis_ref[...], own_ref, left_ref, first)
    for k in range(out_ref.shape[0]):
        out_ref[k] = total


def factor_kernel(parts_ref, own_ref, *rest):
    *left_refs, out_ref = rest
    basis = orthonormal_rows(summed(parts_ref))
    rank, width = basis.shape
    right = right_side(basis)
    out_ref[:, pl.ds(0, width)] = basis
    first = 0
    for left_ref in left_refs:
        for at, size in tiles(left_ref.shape[0], 896):
            difference = planes(left_ref[pl.ds(at, size)] - own_ref[pl.ds(first + at, size)])
            out_ref[:, pl.ds(width + first + at, size)] = columns(difference, right, rank)
        first += left_ref.shape[0]


def change_side(basis):
    b = [x.astype(f32) for x in planes(basis)]
    zero = jnp.zeros_like(b[0])
    return jnp.concatenate([b[0], b[1], b[2], b[0], b[1], b[0], zero, zero], axis=0).astype(bf16)


def change(cols, side):
    c = [x.astype(f32) for x in planes(cols)]
    zero = jnp.zeros_like(cols)
    left = jnp.concatenate([c[0], c[0], c[0], c[1], c[1], c[2], zero, zero], axis=0)
    return dot(jnp.transpose(left).astype(bf16), side)


def half_kernel(message_ref, own_ref, out_ref):
    width = own_ref.shape[1]
    side = change_side(step_size * message_ref[:, pl.ds(0, width)])
    for at, size in tiles(own_ref.shape[0], 896):
        part = pl.ds(at, size)
        out_ref[part] = own_ref[part] + change(message_ref[:, pl.ds(width + at, size)], side)


def final_kernel(message_ref, half_ref, new_ref, cols_ref, held, sems):
    extent, width = half_ref.shape
    copies = [pltpu.make_async_copy(message_ref.at[:, pl.ds(width, extent)], cols_ref, sems.at[0])]
    copies[0].start()
    side = change_side(-step_size * message_ref[:, pl.ds(0, width)])
    for k, (at, size) in enumerate(tiles(extent, 256)):
        part = pl.ds(at, size)
        held[part] = half_ref[part] + change(message_ref[:, pl.ds(width + at, size)], side)
        copies.append(pltpu.make_async_copy(held.at[part], new_ref.at[part], sems.at[1 + k]))
        copies[-1].start()
    for copy in copies:
        copy.wait()


def call(kernel, name, out_shape, out_specs, cost_us, in_specs=None, scratch=(), mib=16):
    return lambda *args: pl.pallas_call(
        kernel,
        out_shape=out_shape,
        in_specs=in_specs or [VMEM] * len(args),
        out_specs=out_specs,
        scratch_shapes=scratch,
        compiler_params=pltpu.CompilerParams(vmem_limit_bytes=mib * 2**20),
        cost_estimate=pl.CostEstimate(flops=int(cost_us * 1.15e9), bytes_accessed=0, transcendentals=0),
        name=name,
    )(*args)


COST = dict(message=2, sum=1, rows=20, basis=14, power=3, factor=3, half=3, final=3)
FIRST = 1792


def shards(weights, warm_q):
    own = weights.T
    start = warm_q[0].T
    rank, extent = start.shape
    width = own.shape[1]
    ranks = lax.axis_size("tensor")
    shape = lambda *dims: jax.ShapeDtypeStruct(dims, f32)
    whole = shape(rank, width + extent)
    held = pltpu.VMEM((extent, width), f32)
    sems = lambda tile: pltpu.SemaphoreType.DMA((1 + len(tiles(extent, tile)),))

    message, own = call(
        message_kernel,
        "message",
        (whole, shape(extent, width)),
        (VMEM, VMEM),
        COST["message"],
        in_specs=[HBM, HBM],
        scratch=[sems(512)],
        mib=51,
    )(start, own)
    left = shifted(message, 1)
    left_first = shifted(own[:FIRST], 1)
    copies = call(rows_kernel, "rows", shape(ranks // 2, rank, width), VMEM, COST["rows"])(left, own)
    along_y = [[2 * y + x for y in range(ranks // 2)] for x in range(2)]
    parts = lax.all_to_all(copies, "tensor", 0, 0, axis_index_groups=along_y, tiled=True)
    rows = call(sum_kernel, "sum", shape(rank, width), VMEM, COST["sum"], mib=4)(parts)
    other = lax.ppermute(rows, "tensor", [(t, t ^ 1) for t in range(ranks)])
    rest, rows = lax.optimization_barrier((own[FIRST:], rows))
    left_rest = shifted(rest, 1)
    both = (shape(rank, width),) * 2
    basis, total = call(basis_kernel, "basis", both, (VMEM, VMEM), COST["basis"])(rows, other, own, left_first)
    copies = call(power_kernel, "power", shape(ranks, rank, width), VMEM, COST["power"])(
        basis, total, own, left_rest
    )
    parts = lax.all_to_all(copies, "tensor", 0, 0, tiled=True)
    factor = call(factor_kernel, "factor", whole, VMEM, COST["factor"])(parts, own, left_first, left_rest)
    right = shifted(factor, -1)
    half = call(half_kernel, "half", shape(extent, width), VMEM, COST["half"])(factor, own)
    new, cols = call(
        final_kernel,
        "final",
        (shape(extent, width), shape(rank, extent)),
        (HBM, HBM),
        COST["final"],
        scratch=[held, sems(256)],
    )(right, half)
    return new.T, cols.T[None]


def solution(mesh):
    in_specs = (P("blk", "tensor"), P("blk", "tensor", None))
    out_specs = (P("blk", "tensor"), P("blk", "tensor", None))
    return jax.shard_map(shards, mesh=mesh, in_specs=in_specs, out_specs=out_specs, check_vma=False)
```

```python
import functools

import jax
import jax.numpy as jnp
from jax import lax
from jax.experimental import pallas as pl
from jax.experimental.pallas import tpu as pltpu
from jax.sharding import PartitionSpec as P

HIGH = lax.Precision.HIGHEST
f32 = jnp.float32
bf16 = jnp.bfloat16
step_size = 0.5
VMEM = pl.BlockSpec(memory_space=pltpu.VMEM)
HBM = pl.BlockSpec(memory_space=pltpu.HBM)
NN = (((1,), (0,)), ((), ()))
NT = (((1,), (1,)), ((), ()))


def shifted(block, distance):
    devices = lax.axis_size("blk")
    return lax.ppermute(block, "blk", [(i, (i + distance) % devices) for i in range(devices)])


def planes(x):
    one = x.astype(bf16)
    rest = x - one.astype(f32)
    two = rest.astype(bf16)
    return one, two, (rest - two.astype(f32)).astype(bf16)


def dot(a, b, dims=NN):
    return lax.dot_general(a, b, dims, preferred_element_type=f32)


def product(small, large):
    rows = small[0].shape[0]
    a = dot(jnp.concatenate(small, axis=0), large[0])
    b = dot(jnp.concatenate(small[:2], axis=0), large[1])
    c = dot(small[0], large[2])
    return a[:rows] + ((a[rows : 2 * rows] + b[:rows]) + (a[2 * rows :] + b[rows:] + c))


def tiles(extent, tile):
    out, at = [], 0
    while at < extent:
        size = extent - at if extent - at <= tile + 128 else tile
        out.append((at, size))
        at += size
    return out


def orthonormal_rows(m):
    rank = m.shape[0]
    g = lax.dot_general(m, m, NT, precision=HIGH, preferred_element_type=f32)
    row = lax.broadcasted_iota(jnp.int32, (rank, 1), 0)
    scale = jnp.ones((rank, 1), f32)
    for j in range(rank):
        pivot = g[j : j + 1, j : j + 1]
        factor = jnp.where(row > j, g[:, j : j + 1] * (1.0 / pivot), 0.0)
        scale = jnp.where(row == j, lax.rsqrt(pivot), scale)
        m = m - factor * m[j : j + 1]
        g = g - factor * g[j : j + 1]
    return m * scale


def summed(parts_ref):
    total = parts_ref[0]
    for k in range(1, parts_ref.shape[0]):
        total = total + parts_ref[k]
    return total


def message_kernel(start_ref, own_ref, out_ref, held, sems):
    rank, extent = start_ref.shape
    width = own_ref.shape[1]
    factor = out_ref.at[:, pl.ds(width, extent)]
    fetch = pltpu.make_async_copy(start_ref, factor, sems.at[0])
    fetch.start()
    copies = []
    for k, (at, size) in enumerate(tiles(extent, 512)):
        part = pl.ds(at, size)
        copies.append((at, size, pltpu.make_async_copy(own_ref.at[part], held.at[part], sems.at[1 + k])))
        copies[-1][2].start()
    fetch.wait()
    total = jnp.zeros((rank, width), f32)
    for at, size, copy in copies:
        copy.wait()
        total = total + product(planes(factor[:, pl.ds(at, size)]), planes(held[pl.ds(at, size)]))
    out_ref[:, pl.ds(0, width)] = total


def cut_kernel(own_ref, out_ref, sems):
    copies = []
    for k, (at, size) in enumerate(tiles(out_ref.shape[0], 768)):
        part = pl.ds(at, size)
        copies.append(pltpu.make_async_copy(own_ref.at[part], out_ref.at[part], sems.at[k]))
        copies[-1].start()
    for copy in copies:
        copy.wait()


def rows_kernel(left_ref, own_ref, out_ref):
    width = own_ref.shape[1]
    rows = left_ref[:, pl.ds(0, width)]
    for at, size in tiles(own_ref.shape[0], 512):
        rows = rows - product(planes(left_ref[:, pl.ds(width + at, size)]), planes(own_ref[pl.ds(at, size)]))
    for k in range(out_ref.shape[0]):
        out_ref[k] = rows


def right_side(basis):
    rank, width = basis.shape
    zero = jnp.zeros((rank, width), f32)
    p = [x.astype(f32) for x in planes(basis)]
    sides = []
    for kept in (3, 2, 1):
        groups = []
        for k in range(4):
            groups += [p[k] if k < kept else zero, zero]
        sides.append(jnp.transpose(jnp.concatenate(groups, axis=0)).astype(bf16))
    return jnp.concatenate(sides, axis=0)


def columns(difference, right, rank):
    groups = jnp.transpose(dot(jnp.concatenate(difference, axis=1), right))
    return groups[:rank] + (groups[2 * rank : 3 * rank] + groups[4 * rank : 5 * rank])


def powered(total, basis, own_ref, left_ref, first):
    rank = basis.shape[0]
    right = right_side(basis)
    for at, size in tiles(left_ref.shape[0], 768):
        difference = planes(left_ref[pl.ds(at, size)] - own_ref[pl.ds(first + at, size)])
        total = total + product(planes(columns(difference, right, rank)), difference)
    return total


def sum_kernel(parts_ref, out_ref):
    out_ref[...] = summed(parts_ref)


def basis_kernel(mine_ref, other_ref, own_ref, left_ref, basis_ref, total_ref):
    basis = orthonormal_rows(mine_ref[...] + other_ref[...])
    basis_ref[...] = basis
    total_ref[...] = powered(jnp.zeros(basis.shape, f32), basis, own_ref, left_ref, 0)


def power_kernel(basis_ref, total_ref, own_ref, left_ref, out_ref):
    first = own_ref.shape[0] - left_ref.shape[0]
    total = powered(total_ref[...], basis_ref[...], own_ref, left_ref, first)
    for k in range(out_ref.shape[0]):
        out_ref[k] = total


def factor_kernel(parts_ref, own_ref, *rest):
    *left_refs, out_ref = rest
    basis = orthonormal_rows(summed(parts_ref))
    rank, width = basis.shape
    right = right_side(basis)
    out_ref[:, pl.ds(0, width)] = basis
    first = 0
    for left_ref in left_refs:
        for at, size in tiles(left_ref.shape[0], 768):
            difference = planes(left_ref[pl.ds(at, size)] - own_ref[pl.ds(first + at, size)])
            out_ref[:, pl.ds(width + first + at, size)] = columns(difference, right, rank)
        first += left_ref.shape[0]


def change_side(basis):
    b = [x.astype(f32) for x in planes(basis)]
    zero = jnp.zeros_like(b[0])
    return jnp.concatenate([b[0], b[1], b[2], b[0], b[1], b[0], zero, zero], axis=0).astype(bf16)


def change(cols, side):
    c = [x.astype(f32) for x in planes(cols)]
    zero = jnp.zeros_like(cols)
    left = jnp.concatenate([c[0], c[0], c[0], c[1], c[1], c[2], zero, zero], axis=0)
    return dot(jnp.transpose(left).astype(bf16), side)


def half_kernel(message_ref, own_ref, out_ref):
    width = own_ref.shape[1]
    side = change_side(step_size * message_ref[:, pl.ds(0, width)])
    for at, size in tiles(own_ref.shape[0], 768):
        part = pl.ds(at, size)
        out_ref[part] = own_ref[part] + change(message_ref[:, pl.ds(width + at, size)], side)


def final_kernel(message_ref, half_ref, new_ref, cols_ref, held, sems):
    extent, width = half_ref.shape
    copies = [pltpu.make_async_copy(message_ref.at[:, pl.ds(width, extent)], cols_ref, sems.at[0])]
    copies[0].start()
    side = change_side(-step_size * message_ref[:, pl.ds(0, width)])
    for k, (at, size) in enumerate(tiles(extent, 256)):
        part = pl.ds(at, size)
        held[part] = half_ref[part] + change(message_ref[:, pl.ds(width + at, size)], side)
        copies.append(pltpu.make_async_copy(held.at[part], new_ref.at[part], sems.at[1 + k]))
        copies[-1].start()
    for copy in copies:
        copy.wait()


def call(kernel, name, out_shape, out_specs, cost_us, in_specs=None, scratch=(), mib=16):
    return lambda *args: pl.pallas_call(
        kernel,
        out_shape=out_shape,
        in_specs=in_specs or [VMEM] * len(args),
        out_specs=out_specs,
        scratch_shapes=scratch,
        compiler_params=pltpu.CompilerParams(vmem_limit_bytes=mib * 2**20),
        cost_estimate=pl.CostEstimate(flops=int(cost_us * 1.15e9), bytes_accessed=0, transcendentals=0),
        name=name,
    )(*args)


COST = dict(message=2, cut=1, sum=1, rows=20, basis=14, power=3, factor=3, half=3, final=3)
FIRST = 1536


def shards(weights, warm_q):
    own = weights.T
    start = warm_q[0].T
    rank, extent = start.shape
    width = own.shape[1]
    ranks = lax.axis_size("tensor")
    shape = lambda *dims: jax.ShapeDtypeStruct(dims, f32)
    whole = shape(rank, width + extent)
    held = pltpu.VMEM((extent, width), f32)
    sems = lambda tile: pltpu.SemaphoreType.DMA((1 + len(tiles(extent, tile)),))

    message = call(
        message_kernel,
        "message",
        whole,
        VMEM,
        COST["message"],
        in_specs=[HBM, HBM],
        scratch=[held, sems(512)],
        mib=62,
    )(start, own)
    own, message = lax.optimization_barrier((own, message))
    left = shifted(message, 1)
    first = call(
        cut_kernel, "cut", shape(FIRST, width), VMEM, COST["cut"], in_specs=[HBM], scratch=[sems(768)], mib=51
    )(own)
    left_first = shifted(first, 1)
    copies = call(rows_kernel, "rows", shape(ranks // 2, rank, width), VMEM, COST["rows"])(left, own)
    along_y = [[2 * y + x for y in range(ranks // 2)] for x in range(2)]
    parts = lax.all_to_all(copies, "tensor", 0, 0, axis_index_groups=along_y, tiled=True)
    rows = call(sum_kernel, "sum", shape(rank, width), VMEM, COST["sum"], mib=4)(parts)
    other = lax.ppermute(rows, "tensor", [(t, t ^ 1) for t in range(ranks)])
    rest, rows = lax.optimization_barrier((own[FIRST:], rows))
    left_rest = shifted(rest, 1)
    both = (shape(rank, width),) * 2
    basis, total = call(basis_kernel, "basis", both, (VMEM, VMEM), COST["basis"])(rows, other, own, left_first)
    copies = call(power_kernel, "power", shape(ranks, rank, width), VMEM, COST["power"])(
        basis, total, own, left_rest
    )
    parts = lax.all_to_all(copies, "tensor", 0, 0, tiled=True)
    factor = call(factor_kernel, "factor", whole, VMEM, COST["factor"])(parts, own, left_first, left_rest)
    right = shifted(factor, -1)
    half = call(half_kernel, "half", shape(extent, width), VMEM, COST["half"])(factor, own)
    new, cols = call(
        final_kernel,
        "final",
        (shape(extent, width), shape(rank, extent)),
        (HBM, HBM),
        COST["final"],
        scratch=[held, sems(256)],
    )(right, half)
    return new.T, cols.T[None]


def solution(mesh):
    in_specs = (P("blk", "tensor"), P("blk", "tensor", None))
    out_specs = (P("blk", "tensor"), P("blk", "tensor", None))
    return jax.shard_map(shards, mesh=mesh, in_specs=in_specs, out_specs=out_specs, check_vma=False)
```

```python
import functools

import jax
import jax.numpy as jnp
from jax import lax
from jax.experimental import pallas as pl
from jax.experimental.pallas import tpu as pltpu
from jax.sharding import PartitionSpec as P

HIGH = lax.Precision.HIGHEST
f32 = jnp.float32
bf16 = jnp.bfloat16
step_size = 0.5
VMEM = pl.BlockSpec(memory_space=pltpu.VMEM)
HBM = pl.BlockSpec(memory_space=pltpu.HBM)
NN = (((1,), (0,)), ((), ()))
NT = (((1,), (1,)), ((), ()))


def shifted(block, distance):
    devices = lax.axis_size("blk")
    return lax.ppermute(block, "blk", [(i, (i + distance) % devices) for i in range(devices)])


def planes(x):
    one = x.astype(bf16)
    rest = x - one.astype(f32)
    two = rest.astype(bf16)
    return one, two, (rest - two.astype(f32)).astype(bf16)


def dot(a, b, dims=NN):
    return lax.dot_general(a, b, dims, preferred_element_type=f32)


def product(small, large):
    rows = small[0].shape[0]
    a = dot(jnp.concatenate(small, axis=0), large[0])
    b = dot(jnp.concatenate(small[:2], axis=0), large[1])
    c = dot(small[0], large[2])
    return a[:rows] + ((a[rows : 2 * rows] + b[:rows]) + (a[2 * rows :] + b[rows:] + c))


def tiles(extent, tile):
    out, at = [], 0
    while at < extent:
        size = extent - at if extent - at <= tile + 128 else tile
        out.append((at, size))
        at += size
    return out


def orthonormal_rows(m):
    rank = m.shape[0]
    g = lax.dot_general(m, m, NT, precision=HIGH, preferred_element_type=f32)
    row = lax.broadcasted_iota(jnp.int32, (rank, 1), 0)
    scale = jnp.ones((rank, 1), f32)
    for j in range(rank):
        pivot = g[j : j + 1, j : j + 1]
        factor = jnp.where(row > j, g[:, j : j + 1] * (1.0 / pivot), 0.0)
        scale = jnp.where(row == j, lax.rsqrt(pivot), scale)
        m = m - factor * m[j : j + 1]
        g = g - factor * g[j : j + 1]
    return m * scale


def summed(parts_ref):
    total = parts_ref[0]
    for k in range(1, parts_ref.shape[0]):
        total = total + parts_ref[k]
    return total


def message_kernel(start_ref, own_ref, out_ref, held, sems):
    rank, extent = start_ref.shape
    width = own_ref.shape[1]
    factor = out_ref.at[:, pl.ds(width, extent)]
    fetch = pltpu.make_async_copy(start_ref, factor, sems.at[0])
    fetch.start()
    copies = []
    for k, (at, size) in enumerate(tiles(extent, 512)):
        part = pl.ds(at, size)
        copies.append((at, size, pltpu.make_async_copy(own_ref.at[part], held.at[part], sems.at[1 + k])))
        copies[-1][2].start()
    fetch.wait()
    total = jnp.zeros((rank, width), f32)
    for at, size, copy in copies:
        copy.wait()
        total = total + product(planes(factor[:, pl.ds(at, size)]), planes(held[pl.ds(at, size)]))
    out_ref[:, pl.ds(0, width)] = total


def rows_kernel(left_ref, own_ref, out_ref):
    width = own_ref.shape[1]
    rows = left_ref[:, pl.ds(0, width)]
    for at, size in tiles(own_ref.shape[0], 512):
        rows = rows - product(planes(left_ref[:, pl.ds(width + at, size)]), planes(own_ref[pl.ds(at, size)]))
    for k in range(out_ref.shape[0]):
        out_ref[k] = rows


def right_side(basis):
    rank, width = basis.shape
    zero = jnp.zeros((rank, width), f32)
    p = [x.astype(f32) for x in planes(basis)]
    sides = []
    for kept in (3, 2, 1):
        groups = []
        for k in range(4):
            groups += [p[k] if k < kept else zero, zero]
        sides.append(jnp.transpose(jnp.concatenate(groups, axis=0)).astype(bf16))
    return jnp.concatenate(sides, axis=0)


def columns(difference, right, rank):
    groups = jnp.transpose(dot(jnp.concatenate(difference, axis=1), right))
    return groups[:rank] + (groups[2 * rank : 3 * rank] + groups[4 * rank : 5 * rank])


def powered(total, basis, own_ref, left_ref, first):
    rank = basis.shape[0]
    right = right_side(basis)
    for at, size in tiles(left_ref.shape[0], 768):
        difference = planes(left_ref[pl.ds(at, size)] - own_ref[pl.ds(first + at, size)])
        total = total + product(planes(columns(difference, right, rank)), difference)
    return total


def sum_kernel(parts_ref, out_ref):
    out_ref[...] = summed(parts_ref)


def basis_kernel(mine_ref, other_ref, own_ref, left_ref, basis_ref, total_ref):
    basis = orthonormal_rows(mine_ref[...] + other_ref[...])
    basis_ref[...] = basis
    total_ref[...] = powered(jnp.zeros(basis.shape, f32), basis, own_ref, left_ref, 0)


def power_kernel(basis_ref, total_ref, own_ref, left_ref, out_ref):
    first = own_ref.shape[0] - left_ref.shape[0]
    total = powered(total_ref[...], basis_ref[...], own_ref, left_ref, first)
    for k in range(out_ref.shape[0]):
        out_ref[k] = total


def factor_kernel(parts_ref, own_ref, *rest):
    *left_refs, out_ref = rest
    basis = orthonormal_rows(summed(parts_ref))
    rank, width = basis.shape
    right = right_side(basis)
    out_ref[:, pl.ds(0, width)] = basis
    first = 0
    for left_ref in left_refs:
        for at, size in tiles(left_ref.shape[0], 768):
            difference = planes(left_ref[pl.ds(at, size)] - own_ref[pl.ds(first + at, size)])
            out_ref[:, pl.ds(width + first + at, size)] = columns(difference, right, rank)
        first += left_ref.shape[0]


def change_side(basis):
    b = [x.astype(f32) for x in planes(basis)]
    zero = jnp.zeros_like(b[0])
    return jnp.concatenate([b[0], b[1], b[2], b[0], b[1], b[0], zero, zero], axis=0).astype(bf16)


def change(cols, side):
    c = [x.astype(f32) for x in planes(cols)]
    zero = jnp.zeros_like(cols)
    left = jnp.concatenate([c[0], c[0], c[0], c[1], c[1], c[2], zero, zero], axis=0)
    return dot(jnp.transpose(left).astype(bf16), side)


def half_kernel(message_ref, own_ref, out_ref):
    width = own_ref.shape[1]
    side = change_side(step_size * message_ref[:, pl.ds(0, width)])
    for at, size in tiles(own_ref.shape[0], 768):
        part = pl.ds(at, size)
        out_ref[part] = own_ref[part] + change(message_ref[:, pl.ds(width + at, size)], side)


def final_kernel(message_ref, half_ref, new_ref, cols_ref, held, sems):
    extent, width = half_ref.shape
    copies = [pltpu.make_async_copy(message_ref.at[:, pl.ds(width, extent)], cols_ref, sems.at[0])]
    copies[0].start()
    side = change_side(-step_size * message_ref[:, pl.ds(0, width)])
    for k, (at, size) in enumerate(tiles(extent, 256)):
        part = pl.ds(at, size)
        held[part] = half_ref[part] + change(message_ref[:, pl.ds(width + at, size)], side)
        copies.append(pltpu.make_async_copy(held.at[part], new_ref.at[part], sems.at[1 + k]))
        copies[-1].start()
    for copy in copies:
        copy.wait()


def call(kernel, name, out_shape, out_specs, cost_us, in_specs=None, scratch=(), mib=16):
    return lambda *args: pl.pallas_call(
        kernel,
        out_shape=out_shape,
        in_specs=in_specs or [VMEM] * len(args),
        out_specs=out_specs,
        scratch_shapes=scratch,
        compiler_params=pltpu.CompilerParams(vmem_limit_bytes=mib * 2**20),
        cost_estimate=pl.CostEstimate(flops=int(cost_us * 1.15e9), bytes_accessed=0, transcendentals=0),
        name=name,
    )(*args)


COST = dict(message=2, sum=1, rows=20, basis=14, power=3, factor=3, half=3, final=3)
FIRST = 1408


def shards(weights, warm_q):
    own = weights.T
    start = warm_q[0].T
    rank, extent = start.shape
    width = own.shape[1]
    ranks = lax.axis_size("tensor")
    shape = lambda *dims: jax.ShapeDtypeStruct(dims, f32)
    whole = shape(rank, width + extent)
    held = pltpu.VMEM((extent, width), f32)
    sems = lambda tile: pltpu.SemaphoreType.DMA((1 + len(tiles(extent, tile)),))

    message = call(
        message_kernel,
        "message",
        whole,
        VMEM,
        COST["message"],
        in_specs=[HBM, HBM],
        scratch=[held, sems(512)],
        mib=60,
    )(start, own)
    own, message = lax.optimization_barrier((own, message))
    left = shifted(message, 1)
    left_first = shifted(own[:FIRST], 1)
    copies = call(rows_kernel, "rows", shape(ranks // 2, rank, width), VMEM, COST["rows"])(left, own)
    along_y = [[2 * y + x for y in range(ranks // 2)] for x in range(2)]
    parts = lax.all_to_all(copies, "tensor", 0, 0, axis_index_groups=along_y, tiled=True)
    rows = call(sum_kernel, "sum", shape(rank, width), VMEM, COST["sum"], mib=4)(parts)
    other = lax.ppermute(rows, "tensor", [(t, t ^ 1) for t in range(ranks)])
    rest, rows = lax.optimization_barrier((own[FIRST:], rows))
    left_rest = shifted(rest, 1)
    both = (shape(rank, width),) * 2
    basis, total = call(basis_kernel, "basis", both, (VMEM, VMEM), COST["basis"])(rows, other, own, left_first)
    copies = call(power_kernel, "power", shape(ranks, rank, width), VMEM, COST["power"])(
        basis, total, own, left_rest
    )
    parts = lax.all_to_all(copies, "tensor", 0, 0, tiled=True)
    factor = call(factor_kernel, "factor", whole, VMEM, COST["factor"])(parts, own, left_first, left_rest)
    right = shifted(factor, -1)
    half = call(half_kernel, "half", shape(extent, width), VMEM, COST["half"])(factor, own)
    new, cols = call(
        final_kernel,
        "final",
        (shape(extent, width), shape(rank, extent)),
        (HBM, HBM),
        COST["final"],
        scratch=[held, sems(256)],
    )(right, half)
    return new.T, cols.T[None]


def solution(mesh):
    in_specs = (P("blk", "tensor"), P("blk", "tensor", None))
    out_specs = (P("blk", "tensor"), P("blk", "tensor", None))
    return jax.shard_map(shards, mesh=mesh, in_specs=in_specs, out_specs=out_specs, check_vma=False)
```
